512 devices in a mesh: view: 4 (over y_lo, core), wide: 128 (over y_hi, x, z).
Axes of the slice: x: 4, y: 4 (y_hi: 2, y_lo: 2; y = y_hi * 2 + y_lo), z: 16, core: 2. Of those that a mesh axis runs over, the one named last changes fastest.
Arguments:
- estimate: float32 [128, 512, 384], P('wide'), may hold values from 0.5 to 2
- observed: float32 [4, 128, 512, 384], P('view', None, 'wide'), may hold values from 0.25 to 4
- psf_x: float32 [4, 63], P('view'), may hold values from 0.01 to 1
- psf_y: float32 [4, 63], P('view'), may hold values from 0.01 to 1
- psf_z: float32 [4, 63], P('view'), may hold values from 0.01 to 1
Outputs:
- refined: float32 [128, 512, 384], P('wide')
The draws below stay inside these ranges and needn't reach their ends.
All inputs are finite; a program needn't handle non-finite values.
Results may differ from the reference program's by a relative error of at most 0.0001.
Values sent between devices are 32-bit elements; how exact they have to be, the bound alone decides.
A program may use at most 64 MiB of HBM per device.

```python
import math
import jax
import jax.numpy as jnp
from jax import lax

X = 512
Y = 384
TAPS = 63
ITERS = 2
VIEWS = 4
NZ = 128


def draw_psf_x(key, part):
    key = jax.random.fold_in(key, 11)
    tail_key, peak_key = jax.random.split(key)
    tail_values = jnp.exp(jax.random.uniform(tail_key, (VIEWS, TAPS), jnp.float32, math.log(0.01), math.log(0.05)))
    peak_value = jnp.exp(jax.random.uniform(peak_key, (VIEWS, 1), jnp.float32, math.log(0.5), 0.0))
    centre_mask = (jnp.arange(TAPS) == (TAPS - 1) // 2)[None, :]
    return jnp.clip(jnp.where(centre_mask, peak_value, tail_values), 0.01, 1.0)


def draw_psf_y(key, part):
    key = jax.random.fold_in(key, 12)
    tail_key, peak_key = jax.random.split(key)
    tail_values = jnp.exp(jax.random.uniform(tail_key, (VIEWS, TAPS), jnp.float32, math.log(0.01), math.log(0.05)))
    peak_value = jnp.exp(jax.random.uniform(peak_key, (VIEWS, 1), jnp.float32, math.log(0.5), 0.0))
    centre_mask = (jnp.arange(TAPS) == (TAPS - 1) // 2)[None, :]
    return jnp.clip(jnp.where(centre_mask, peak_value, tail_values), 0.01, 1.0)


def draw_psf_z(key, part):
    key = jax.random.fold_in(key, 13)
    tail_key, peak_key = jax.random.split(key)
    tail_values = jnp.exp(jax.random.uniform(tail_key, (VIEWS, TAPS), jnp.float32, math.log(0.01), math.log(0.05)))
    peak_value = jnp.exp(jax.random.uniform(peak_key, (VIEWS, 1), jnp.float32, math.log(0.5), 0.0))
    centre_mask = (jnp.arange(TAPS) == (TAPS - 1) // 2)[None, :]
    return jnp.clip(jnp.where(centre_mask, peak_value, tail_values), 0.01, 1.0)


def block_levels(rng, shape, cuts, least, high):
    loudness, own = 1.0, jax.random.fold_in(rng, 6)
    for position, parts in cuts:
        steps = jnp.exp(jax.random.uniform(jax.random.fold_in(own, position), (parts,), jnp.float32, least / len(cuts), high / len(cuts)))
        loudness = loudness * jnp.repeat(steps, shape[position] // parts).reshape([-1 if axis == position else 1 for axis in range(len(shape))])
    return loudness


def setup_inputs(seed: int = 0) -> dict:
    key_list = jax.random.split(jax.random.key(seed), 6)
    return {
        "estimate": jnp.clip(jnp.exp(math.log(2.0) - 1.3862944 * jax.random.uniform(key_list[0], (NZ, X, Y), jnp.float32) ** block_levels(key_list[0], (NZ, X, Y), ((0, 128),), -0.2, 0.2)), 0.5, 2.0),
        "observed": jnp.clip(jnp.exp(math.log(4.0) - 2.7725887 * jax.random.uniform(key_list[1], (VIEWS, NZ, X, Y), jnp.float32) ** block_levels(key_list[1], (VIEWS, NZ, X, Y), ((0, 4), (2, 128)), -0.2, 0.2)), 0.25, 4.0),
        "psf_x": draw_psf_x(jax.random.fold_in(key_list[5], 71), 0),
        "psf_y": draw_psf_y(jax.random.fold_in(key_list[5], 71), 0),
        "psf_z": draw_psf_z(jax.random.fold_in(key_list[5], 71), 0),
    }


def band_matrix(tap_values, count):
    weights = tap_values / jnp.sum(tap_values)
    cell_index = jnp.arange(count, dtype=jnp.int32)
    offset = cell_index[:, None] - cell_index[None, :] + (TAPS - 1) // 2
    inside = (offset >= 0) & (offset < TAPS)
    picked = jnp.take(weights, jnp.clip(offset, 0, TAPS - 1).astype(jnp.int32))
    return jnp.where(inside, picked, jnp.zeros_like(picked))


def reference(estimate, observed, psf_x, psf_y, psf_z):
    high = lax.Precision.HIGHEST
    current = estimate
    for iteration in range(ITERS):
        summed = jnp.zeros_like(current)
        for viewer in range(VIEWS):
            kern_x = band_matrix(psf_x[viewer], X)
            kern_y = band_matrix(psf_y[viewer], Y)
            kern_z = band_matrix(psf_z[viewer], NZ)
            plane = jnp.einsum("zxy,wy->zxw", current, kern_y, precision=high)
            plane = jnp.einsum("vx,zxy->zvy", kern_x, plane, precision=high)
            blurred = jnp.einsum("wz,zxy->wxy", kern_z, plane, precision=high)
            quotient = observed[viewer] / blurred
            back_proj = jnp.einsum("zw,zxy->wxy", kern_z, quotient, precision=high)
            back_proj = jnp.einsum("xv,zxy->zvy", kern_x, back_proj, precision=high)
            correction = jnp.einsum("zxy,yw->zxw", back_proj, kern_y, precision=high)
            summed = summed + correction
        current = current * summed / VIEWS
    return current
```

```python
import functools

import jax
import jax.numpy as jnp
from jax import lax
from jax.experimental import pallas as pl
from jax.experimental.pallas import tpu as pltpu
from jax.sharding import PartitionSpec as P

TAPS = 63
HALF = (TAPS - 1) // 2
ITERS = 2
MESH = pl.DeviceIdType.MESH
F32 = jnp.float32
BF16 = jnp.bfloat16

RING = 16
GROUPS = 8
Q = 4
PLANE = GROUPS * Q
J = 4
Y = 384
NZ = 128
ROWS = PLANE * Q * J


def iota(shape, axis):
    return lax.broadcasted_iota(jnp.int32, shape, axis)


def split(value):
    top = value.astype(BF16)
    return top, (value - top.astype(F32)).astype(BF16)


def dot(a, b):
    return jnp.dot(a, b, preferred_element_type=F32)


def dot3(a_top, a_low, b_top, b_low):
    return dot(a_top, b_top) + (dot(a_top, b_low) + dot(a_low, b_top))


def toeplitz(row, rows, width, first):
    full = width + 128
    wide = jnp.concatenate([row, jnp.zeros((1, full - 128), F32)], axis=1)
    spread = jnp.broadcast_to(wide, (rows, full))
    return pltpu.roll(spread, first % full, axis=1, stride=1, stride_axis=0)[:, :width]


def kernel(
    est, obs, psf, out,
    taps, mh, ml, mth, mtl, nh, nl, nth, ntl, kyh, kyl, kyth, kytl,
    u, s1, r1, s2, r2, back, rh, rl, wh, wl, blur, o1, o2, ob, slab,
    psf_s, psf_r, uin_s, uin_r, halo_s, halo_r, a1_s, a1_r, a2_s, a2_r, bk_s, bk_r,
    o1_s, o1_r, o2_s, o2_r, o3_s, o3_r, uo_s, uo_r, fw_s, fa_r, fb_r,
):
    q = lax.axis_index("view")
    w = lax.axis_index("wide")
    h = w // RING
    zc = w % RING
    p = h * Q + q

    def dev(hh, zz, qq):
        return {"view": qq, "wide": hh * RING + zz}

    def remote(src, dst, send, recv, where):
        return pltpu.make_async_remote_copy(
            src_ref=src, dst_ref=dst, send_sem=send, recv_sem=recv, device_id=where, device_id_type=MESH
        )

    def wait_for(ref, sem):
        pltpu.make_async_copy(ref, ref, sem).wait()

    def loop(low, high, body):
        lax.fori_loop(low, high, lambda i, c: (body(i), c)[1], 0)

    barrier = pltpu.get_barrier_semaphore()

    def greet_ring(d):
        pl.semaphore_signal(barrier, inc=1, device_id=dev(h, (zc + d) % RING, q), device_id_type=MESH)

    def greet_plane(d):
        other = (p + d) % PLANE
        pl.semaphore_signal(barrier, inc=1, device_id=dev(other // Q, zc, other % Q), device_id_type=MESH)

    loop(1, RING, greet_ring)
    loop(1, PLANE, greet_plane)
    pl.semaphore_wait(barrier, RING - 1 + PLANE - 1)

    def send_taps(d):
        remote(psf, taps.at[q], psf_s, psf_r, dev(h, zc, (q + d) % Q)).start()

    loop(1, Q, send_taps)
    pltpu.make_async_copy(psf, taps.at[q], psf_r).start()

    owner = zc % Q == q

    @pl.when(owner)
    def _():
        def send(d):
            t = (zc + d) % RING
            remote(est.at[pl.ds(t * 32, 32)], u.at[0, 1, pl.ds((zc // 4) * 32, 32)], uin_s, uin_r, dev(h, t, q)).start()

        loop(1, RING, send)
        pltpu.make_async_copy(est.at[pl.ds(zc * 32, 32)], u.at[0, 1, pl.ds((zc // 4) * 32, 32)], uin_r).start()

    def obs_first(d):
        c = (h + d) % GROUPS
        remote(obs.at[:, pl.ds(c * 16, 16)], o1.at[h], o1_s, o1_r.at[h], dev(c, zc, q)).start()

    loop(1, GROUPS, obs_first)
    pltpu.make_async_copy(obs.at[:, pl.ds(h * 16, 16)], o1.at[h], o1_r.at[h]).start()

    wait_for(taps, psf_r)

    norm = []
    for v in range(Q):
        raw = taps[v]
        norm.append(raw / jnp.sum(raw, axis=1, keepdims=True))

    def row_of(v, r):
        return norm[v][r : r + 1, :]

    low_ok = zc != 0
    high_ok = zc != RING - 1
    t_mat = jnp.concatenate([toeplitz(row_of(v, 3), 32, 128, 1) for v in range(Q)], axis=0)
    k_lane = iota((128, 128), 1)
    t_mat = jnp.where(((k_lane >= 32) | low_ok) & ((k_lane < 64) | high_ok), t_mat, 0.0)
    k_row = iota((128, 128), 0)
    tt_mat = jnp.zeros((128, 128), F32)
    for v in range(Q):
        block = toeplitz(row_of(v, 0), 128, 128, 32 * v - 63)
        tt_mat = jnp.where(k_lane // 32 == v, block, tt_mat)
    tt_mat = jnp.where(((k_row >= 32) | low_ok) & ((k_row < 64) | high_ok), tt_mat, 0.0)
    t_top, t_low = split(t_mat)
    tt_top, tt_low = split(tt_mat)
    r_row, r_lane = iota((ROWS, 128), 0), iota((ROWS, 128), 1)
    pick_rows = (((r_row // 16) + 32 * ((r_row // 4) % 4)) == r_lane).astype(F32).astype(BF16)
    c_row, c_lane = iota((128, Y), 0), iota((128, Y), 1)
    pick_cols = ((c_lane // 128) * 32 + c_lane % 32 == c_row).astype(F32).astype(BF16)
    same_j = (iota((ROWS, Y), 0) % 4) == ((iota((ROWS, Y), 1) // 32) % 4)
    for part, ref in ((t_top, mh), (t_low, ml)):
        rows = dot(pick_rows, part).astype(BF16)
        ref[...] = jnp.where(same_j, dot(rows, pick_cols), 0.0).astype(BF16)
    rt_row, rt_lane = iota((128, ROWS), 0), iota((128, ROWS), 1)
    pick_rows_t = (((rt_lane // 16) + 32 * ((rt_lane // 4) % 4)) == rt_row).astype(F32).astype(BF16)
    ct_row, ct_lane = iota((Y, 128), 0), iota((Y, 128), 1)
    pick_cols_t = ((ct_row // 128) * 32 + ct_row % 32 == ct_lane).astype(F32).astype(BF16)
    same_j_t = (iota((Y, ROWS), 1) % 4) == ((iota((Y, ROWS), 0) // 32) % 4)
    for part, ref in ((tt_top, mth), (tt_low, mtl)):
        rows = dot(pick_cols_t, part).astype(BF16)
        ref[...] = jnp.where(same_j_t, dot(rows, pick_rows_t), 0.0).astype(BF16)
    g_row, g_lane = iota((128, ROWS), 0), iota((128, ROWS), 1)
    g_pick = ((g_lane // 64) * 16 + (g_lane % 4) * 4 + (g_lane // 16) % 4) == g_row
    gt_row, gt_lane = iota((ROWS, 128), 0), iota((ROWS, 128), 1)
    gt_pick = ((gt_row // 64) * 16 + (gt_row % 4) * 4 + (gt_row // 16) % 4) == gt_lane
    for v in range(Q):
        chosen = (g_pick & ((g_lane // 4) % 4 == v)).astype(F32).astype(BF16)
        top, low = split(toeplitz(row_of(v, 5), NZ, NZ, -HALF))
        nh[v] = dot(top, chosen).astype(BF16)
        nl[v] = dot(low, chosen).astype(BF16)
        chosen = (gt_pick & ((gt_row // 4) % 4 == v)).astype(F32).astype(BF16)
        top, low = split(toeplitz(row_of(v, 2), NZ, NZ, -HALF))
        nth[:, v * NZ : (v + 1) * NZ] = dot(chosen, top).astype(BF16)
        ntl[:, v * NZ : (v + 1) * NZ] = dot(chosen, low).astype(BF16)
        top, low = split(toeplitz(row_of(v, 1), Y, Y, -HALF))
        kyth[v] = top
        kytl[v] = low
        top, low = split(toeplitz(row_of(v, 4), Y, Y, -HALF))
        kyh[v] = top
        kyl[v] = low

    def send_plane(send_buf, recv_buf, send, recv, chunk):
        def one(k):
            other = chunk * 8 + k

            @pl.when(other != p)
            def _():
                remote(send_buf.at[other], recv_buf.at[p], send, recv, dev(other // Q, zc, other % Q)).start()

            @pl.when(other == p)
            def _():
                pltpu.make_async_copy(send_buf.at[other], recv_buf.at[p], recv).start()

        loop(0, 8, one)

    left = (zc + RING - 1) % RING
    right = (zc + 1) % RING

    for it in range(ITERS):
        if it == 0:
            wait_for(u.at[0, 1], uin_r)
        remote(u.at[it, 1], u.at[it, 2], halo_s.at[it, 0], halo_r.at[it, 0], dev(h, left, q)).start()
        remote(u.at[it, 1], u.at[it, 0], halo_s.at[it, 1], halo_r.at[it, 1], dev(h, right, q)).start()

        if it == 0:
            a = zc // 8
            b = zc % 8

            def obs_second(d):
                hs = (h + d) % GROUPS
                t = 2 * hs + a
                wait_for(o1.at[hs], o1_r.at[hs])

                @pl.when(t != zc)
                def _():
                    remote(o1.at[hs], o2.at[b], o2_s, o2_r.at[b], dev(h, t, q)).start()

                @pl.when(t == zc)
                def _():
                    pltpu.make_async_copy(o1.at[hs], o2.at[b], o2_r.at[b]).start()

            loop(0, GROUPS, obs_second)

        wait_for(u.at[it, 2], halo_r.at[it, 0])
        wait_for(u.at[it, 0], halo_r.at[it, 1])

        u_top, u_low = split(u[it].reshape(3 * NZ, Y))
        rh[0 : 3 * NZ] = u_top
        rl[0 : 3 * NZ] = u_low

        def forward(c):
            at = pl.ds(pl.multiple_of(c * 128, 128), 128)
            got = dot3(mh[at], ml[at], rh[0 : 3 * NZ], rl[0 : 3 * NZ])
            s1[it, pl.ds(c * 8, 8)] = got.reshape(8, 16, Y)
            send_plane(s1.at[it], r1.at[it], a1_s.at[it], a1_r.at[it], c)

        loop(0, 4, forward)
        wait_for(r1.at[it], a1_r.at[it])

        r_top, r_low = split(r1[it].reshape(ROWS, Y))
        rh[...] = r_top
        rl[...] = r_low

        def blur_view(v):
            z_top, z_low = split(dot3(nh[v], nl[v], rh[...], rl[...]))
            blur[v] = dot3(z_top, z_low, kyth[v], kytl[v])

        loop(0, Q, blur_view)

        if it == 0:
            def obs_third(b):
                wait_for(o2.at[b], o2_r.at[b])

                def one(i):
                    mine = (b == h) & (i == q)
                    dst = ob.at[q, pl.ds(h * 16, 16)]

                    @pl.when(jnp.logical_not(mine))
                    def _():
                        remote(o2.at[b, i], dst, o3_s, o3_r, dev(b, zc, i)).start()

                    @pl.when(mine)
                    def _():
                        pltpu.make_async_copy(o2.at[b, i], dst, o3_r).start()

                loop(0, Q, one)

            loop(0, GROUPS, obs_third)
            wait_for(ob, o3_r)

        def back_view(v):
            q_top, q_low = split(ob[v] / blur[v])
            w_top, w_low = split(dot3(q_top, q_low, kyh[v], kyl[v]))
            wh[pl.ds(pl.multiple_of(v * NZ, NZ), NZ)] = w_top
            wl[pl.ds(pl.multiple_of(v * NZ, NZ), NZ)] = w_low

        loop(0, Q, back_view)

        def backward(c):
            at = pl.ds(pl.multiple_of(c * 128, 128), 128)
            got = dot3(nth[at], ntl[at], wh[...], wl[...])
            s2[it, pl.ds(c * 8, 8)] = got.reshape(8, 16, Y)
            send_plane(s2.at[it], r2.at[it], a2_s.at[it], a2_r.at[it], c)

        loop(0, 4, backward)
        wait_for(r2.at[it], a2_r.at[it])

        r_top, r_low = split(r2[it].reshape(ROWS, Y))
        rh[...] = r_top
        rl[...] = r_low

        def piece(k):
            return dot3(mth[k * NZ : (k + 1) * NZ], mtl[k * NZ : (k + 1) * NZ], rh[...], rl[...])

        back[it, 0] = piece(0)
        remote(back.at[it, 0], back.at[it, 4], bk_s.at[it, 0], bk_r.at[it, 0], dev(h, left, q)).start()
        back[it, 2] = piece(2)
        remote(back.at[it, 2], back.at[it, 3], bk_s.at[it, 1], bk_r.at[it, 1], dev(h, right, q)).start()
        mine = piece(1)
        wait_for(back.at[it, 4], bk_r.at[it, 0])
        wait_for(back.at[it, 3], bk_r.at[it, 1])
        u[it + 1, 1] = u[it, 1] * (mine + back[it, 3] + back[it, 4]) * (1.0 / Q)

    def send_out(j):
        t = 4 * j + q
        src = u.at[ITERS, 1, pl.ds(j * 32, 32)]
        dst = slab.at[pl.ds(zc * 32, 32)]

        @pl.when(t != zc)
        def _():
            remote(src, dst, uo_s, uo_r.at[zc], dev(h, t, q)).start()

        @pl.when(t == zc)
        def _():
            pltpu.make_async_copy(src, dst, uo_r.at[zc]).start()

    loop(0, J, send_out)
    home = zc % Q
    role = q ^ home

    @pl.when(role == 0)
    def _():
        def forward_out(d):
            t = (zc + d) % RING
            at = pl.ds(t * 32, 32)
            wait_for(slab.at[at], uo_r.at[t])
            remote(slab.at[at], slab.at[at], fw_s.at[0], fa_r.at[t], dev(h, zc, q ^ 2)).start()
            remote(slab.at[at], slab.at[at], fw_s.at[1], fb_r.at[t], dev(h, zc, q ^ 1)).start()

        loop(0, RING, forward_out)
        wait_for(slab, fw_s.at[0])
        wait_for(slab, fw_s.at[1])

    @pl.when(role == 2)
    def _():
        def forward_again(d):
            t = (zc + d) % RING
            at = pl.ds(t * 32, 32)
            wait_for(slab.at[at], fa_r.at[t])
            remote(slab.at[at], slab.at[at], fw_s.at[1], fb_r.at[t], dev(h, zc, q ^ 1)).start()

        loop(0, RING, forward_again)
        wait_for(slab, fw_s.at[1])

    @pl.when((role == 1) | (role == 3))
    def _():
        def last(t):
            wait_for(slab.at[pl.ds(t * 32, 32)], fb_r.at[t])

        loop(0, RING, last)

    out[0] = slab[...]

    @pl.when(owner)
    def _():
        wait_for(est.at[pl.ds(0, 480)], uin_s)

    def wait_bytes(count, ref, sem):
        loop(0, count, lambda i: wait_for(ref, sem))

    wait_bytes(Q - 1, psf, psf_s)
    wait_for(o1.at[pl.ds(0, GROUPS - 1)], o1_s)
    kept2 = (zc % 2 == zc // 8).astype(jnp.int32)
    wait_bytes(GROUPS - kept2, o1.at[0], o2_s)
    wait_for(s1.at[0, pl.ds(0, PLANE - 1)], o3_s)
    for it in range(ITERS):
        for k in range(2):
            wait_for(u.at[it, 1], halo_s.at[it, k])
            wait_for(back.at[it, 0], bk_s.at[it, k])
        wait_for(s1.at[it, pl.ds(0, PLANE - 1)], a1_s.at[it])
        wait_for(s2.at[it, pl.ds(0, PLANE - 1)], a2_s.at[it])
    kept = (zc % Q == q).astype(jnp.int32)
    wait_bytes(J - kept, slab.at[pl.ds(0, 32)], uo_s)


def per_device(estimate, observed, psf_x, psf_y, psf_z):
    rows = jnp.concatenate([psf_x, psf_y, psf_z], axis=0)
    rows = jnp.concatenate([rows, jnp.flip(rows, axis=1)], axis=0)
    psf = jnp.pad(rows, ((0, 2), (0, 128 - TAPS)))
    recorded = jnp.transpose(observed[0], (1, 0, 2))
    vmem = pl.BlockSpec(memory_space=pltpu.VMEM)
    sem = pltpu.SemaphoreType.DMA
    return pl.pallas_call(
        kernel,
        out_shape=jax.ShapeDtypeStruct((1, 512, Y), F32),
        in_specs=[vmem] * 3,
        out_specs=vmem,
        scratch_shapes=[
            pltpu.VMEM((Q, 8, 128), F32),
            pltpu.VMEM((ROWS, Y), BF16),
            pltpu.VMEM((ROWS, Y), BF16),
            pltpu.VMEM((Y, ROWS), BF16),
            pltpu.VMEM((Y, ROWS), BF16),
            pltpu.VMEM((Q, NZ, ROWS), BF16),
            pltpu.VMEM((Q, NZ, ROWS), BF16),
            pltpu.VMEM((ROWS, Q * NZ), BF16),
            pltpu.VMEM((ROWS, Q * NZ), BF16),
            pltpu.VMEM((Q, Y, Y), BF16),
            pltpu.VMEM((Q, Y, Y), BF16),
            pltpu.VMEM((Q, Y, Y), BF16),
            pltpu.VMEM((Q, Y, Y), BF16),
            pltpu.VMEM((ITERS + 1, 3, NZ, Y), F32),
            pltpu.VMEM((ITERS, PLANE, 16, Y), F32),
            pltpu.VMEM((ITERS, PLANE, 16, Y), F32),
            pltpu.VMEM((ITERS, PLANE, 16, Y), F32),
            pltpu.VMEM((ITERS, PLANE, 16, Y), F32),
            pltpu.VMEM((ITERS, 5, NZ, Y), F32),
            pltpu.VMEM((ROWS, Y), BF16),
            pltpu.VMEM((ROWS, Y), BF16),
            pltpu.VMEM((ROWS, Y), BF16),
            pltpu.VMEM((ROWS, Y), BF16),
            pltpu.VMEM((Q, NZ, Y), F32),
            pltpu.VMEM((GROUPS, 4, 16, Y), F32),
            pltpu.VMEM((GROUPS, 4, 16, Y), F32),
            pltpu.VMEM((Q, NZ, Y), F32),
            pltpu.VMEM((512, Y), F32),
            sem, sem,
            sem, sem,
            sem((ITERS, 2)), sem((ITERS, 2)),
            sem((ITERS,)), sem((ITERS,)),
            sem((ITERS,)), sem((ITERS,)),
            sem((ITERS, 2)), sem((ITERS, 2)),
            sem, sem((GROUPS,)),
            sem, sem((GROUPS,)),
            sem, sem,
            sem, sem((RING,)),
            sem((2,)), sem((RING,)), sem((RING,)),
        ],
        compiler_params=pltpu.CompilerParams(
            collective_id=0, has_side_effects=True, vmem_limit_bytes=48 * 1024 * 1024
        ),
    )(estimate[0], recorded, psf)


def solution(mesh):
    return jax.shard_map(
        per_device,
        mesh=mesh,
        in_specs=(
            P("wide", None, None),
            P("view", None, "wide", None),
            P("view", None),
            P("view", None),
            P("view", None),
        ),
        out_specs=P("wide", None, None),
        check_vma=False,
    )
```

```python
import functools

import jax
import jax.numpy as jnp
from jax import lax
from jax.experimental import pallas as pl
from jax.experimental.pallas import tpu as pltpu
from jax.sharding import PartitionSpec as P

TAPS = 63
HALF = (TAPS - 1) // 2
ITERS = 2
MESH = pl.DeviceIdType.MESH
F32 = jnp.float32
BF16 = jnp.bfloat16

RING = 16
GROUPS = 8
Q = 4
PLANE = GROUPS * Q
J = 4
Y = 384
NZ = 128
LANES = 128
CHUNKS = Y // LANES
ROWS = PLANE * Q * J


def iota(shape, axis):
    return lax.broadcasted_iota(jnp.int32, shape, axis)


def split(value):
    top = value.astype(BF16)
    return top, (value - top.astype(F32)).astype(BF16)


def dot(a, b):
    return jnp.dot(a, b, preferred_element_type=F32)


def dot3(a_top, a_low, b_top, b_low):
    return dot(a_top, b_top) + (dot(a_top, b_low) + dot(a_low, b_top))


def toeplitz(row, rows, width, first):
    full = width + 128
    wide = jnp.concatenate([row, jnp.zeros((1, full - 128), F32)], axis=1)
    spread = jnp.broadcast_to(wide, (rows, full))
    return pltpu.roll(spread, first % full, axis=1, stride=1, stride_axis=0)[:, :width]


def kernel(
    est, obs, psf, out,
    taps, mh, ml, mth, mtl, nh, nl, nth, ntl, kyh, kyl, kyth, kytl,
    u, s1, r1, s2, r2, back, xb, zb, ztop, zlow, wb, o1, o2, ob,
    psf_s, psf_r, uin_s, uin_r, halo_s, halo_r, a1_s, a1_r, a2_s, a2_r, bk_s, bk_r,
    o1_s, o1_r, o2_s, o2_r, o3_s, o3_r, uo_s, uo_r, fw_s, fa_r, fb_r,
):
    q = lax.axis_index("view")
    w = lax.axis_index("wide")
    h = w // RING
    zc = w % RING
    p = h * Q + q

    def dev(hh, zz, qq):
        return {"view": qq, "wide": hh * RING + zz}

    def remote(src, dst, send, recv, where):
        return pltpu.make_async_remote_copy(
            src_ref=src, dst_ref=dst, send_sem=send, recv_sem=recv, device_id=where, device_id_type=MESH
        )

    def wait_for(ref, sem):
        pltpu.make_async_copy(ref, ref, sem).wait()

    def loop(low, high, body):
        lax.fori_loop(low, high, lambda i, c: (body(i), c)[1], 0)

    barrier = pltpu.get_barrier_semaphore()

    def greet_ring(d):
        pl.semaphore_signal(barrier, inc=1, device_id=dev(h, (zc + d) % RING, q), device_id_type=MESH)

    def greet_plane(d):
        other = (p + d) % PLANE
        pl.semaphore_signal(barrier, inc=1, device_id=dev(other // Q, zc, other % Q), device_id_type=MESH)

    loop(1, RING, greet_ring)
    loop(1, PLANE, greet_plane)
    pl.semaphore_wait(barrier, RING - 1 + PLANE - 1)

    def wait_bytes(count, ref, sem):
        loop(0, count, lambda i: wait_for(ref, sem))

    drains = []
    owner = zc % Q == q
    left = (zc + RING - 1) % RING
    right = (zc + 1) % RING

    def partner(k):
        step = k // 2
        x = (h + step) % 4
        y = (h // 4 * 2 + q // 2 + step // 4 + step) % 4
        return (y // 2 * 4 + x) * Q + y % 2 * 2 + (q + k) % 2

    def send_plane(send_buf, recv_buf, send, recv, first, count):
        def one(i):
            k = first + i
            other = partner(k)

            @pl.when(k != 0)
            def _():
                remote(send_buf.at[k], recv_buf.at[p], send, recv, dev(other // Q, zc, other % Q)).start()

            @pl.when(k == 0)
            def _():
                pltpu.make_async_copy(send_buf.at[k], recv_buf.at[p], recv).start()

        loop(0, count, one)

    def lanes(c):
        return pl.ds(c * LANES, LANES)

    def pair(ref, value):
        top, low = split(value)
        ref[:, 0:LANES] = top
        ref[:, LANES:] = low

    def times_pair(a_top, a_low, ref):
        got = dot(a_top, ref[...])
        return got[:, 0:LANES] + (got[:, LANES:] + dot(a_low, ref[:, 0:LANES]))

    def taps_out():
        def send_taps(d):
            remote(psf, taps.at[q], psf_s, psf_r, dev(h, zc, (q + d) % Q)).start()

        loop(1, Q, send_taps)
        pltpu.make_async_copy(psf, taps.at[q], psf_r).start()
        drains.append(lambda: wait_bytes(Q - 1, psf, psf_s))

    def estimate_in():
        @pl.when(owner)
        def _():
            for c in range(CHUNKS):
                mine = u.at[0, c, 1, pl.ds((zc // 4) * 32, 32)]

                def send(i):
                    t = (zc + 8 + (1 - 2 * (i % 2)) * (i // 2)) % RING
                    remote(est.at[pl.ds(t * 32, 32), lanes(c)], mine, uin_s, uin_r.at[c], dev(h, t, q)).start()

                loop(1, RING, send)
                pltpu.make_async_copy(est.at[pl.ds(zc * 32, 32), lanes(c)], mine, uin_r.at[c]).start()

        def drain():
            @pl.when(owner)
            def _():
                wait_for(est.at[pl.ds(0, 480)], uin_s)

        drains.append(drain)

    def estimate_wait(c):
        wait_for(u.at[0, c, 1], uin_r.at[c])

    def observed_first():
        def obs_first(d):
            c = (h + d) % GROUPS
            remote(obs.at[:, pl.ds(c * 16, 16)], o1.at[h], o1_s, o1_r.at[h], dev(c, zc, q)).start()

        loop(1, GROUPS, obs_first)
        pltpu.make_async_copy(obs.at[:, pl.ds(h * 16, 16)], o1.at[h], o1_r.at[h]).start()
        drains.append(lambda: wait_for(o1.at[pl.ds(0, GROUPS - 1)], o1_s))

    def matrices():
        wait_for(taps, psf_r)

        norm = []
        for v in range(Q):
            raw = taps[v]
            norm.append(raw / jnp.sum(raw, axis=1, keepdims=True))

        def row_of(v, r):
            return norm[v][r : r + 1, :]

        low_ok = zc != 0
        high_ok = zc != RING - 1
        t_mat = jnp.concatenate([toeplitz(row_of(v, 3), 32, 128, 1) for v in range(Q)], axis=0)
        k_lane = iota((128, 128), 1)
        t_mat = jnp.where(((k_lane >= 32) | low_ok) & ((k_lane < 64) | high_ok), t_mat, 0.0)
        k_row = iota((128, 128), 0)
        tt_mat = jnp.zeros((128, 128), F32)
        for v in range(Q):
            block = toeplitz(row_of(v, 0), 128, 128, 32 * v - 63)
            tt_mat = jnp.where(k_lane // 32 == v, block, tt_mat)
        tt_mat = jnp.where(((k_row >= 32) | low_ok) & ((k_row < 64) | high_ok), tt_mat, 0.0)
        t_top, t_low = split(t_mat)
        tt_top, tt_low = split(tt_mat)
        r_row, r_lane = iota((ROWS, 128), 0), iota((ROWS, 128), 1)
        pick_rows = ((partner(r_row // 16) + 32 * ((r_row // 4) % 4)) == r_lane).astype(F32).astype(BF16)
        c_row, c_lane = iota((128, Y), 0), iota((128, Y), 1)
        pick_cols = ((c_lane // 128) * 32 + c_lane % 32 == c_row).astype(F32).astype(BF16)
        same_j = (iota((ROWS, Y), 0) % 4) == ((iota((ROWS, Y), 1) // 32) % 4)
        for part, ref in ((t_top, mh), (t_low, ml)):
            rows = dot(pick_rows, part).astype(BF16)
            ref[...] = jnp.where(same_j, dot(rows, pick_cols), 0.0).astype(BF16)
        rt_row, rt_lane = iota((128, ROWS), 0), iota((128, ROWS), 1)
        pick_rows_t = (((rt_lane // 16) + 32 * ((rt_lane // 4) % 4)) == rt_row).astype(F32).astype(BF16)
        ct_row, ct_lane = iota((Y, 128), 0), iota((Y, 128), 1)
        pick_cols_t = ((ct_row // 128) * 32 + ct_row % 32 == ct_lane).astype(F32).astype(BF16)
        same_j_t = (iota((Y, ROWS), 1) % 4) == ((iota((Y, ROWS), 0) // 32) % 4)
        for part, ref in ((tt_top, mth), (tt_low, mtl)):
            rows = dot(pick_cols_t, part).astype(BF16)
            ref[...] = jnp.where(same_j_t, dot(rows, pick_rows_t), 0.0).astype(BF16)
        g_row, g_lane = iota((128, ROWS), 0), iota((128, ROWS), 1)
        g_pick = ((g_lane // 64) * 16 + (g_lane % 4) * 4 + (g_lane // 16) % 4) == g_row
        gt_row, gt_lane = iota((ROWS, 128), 0), iota((ROWS, 128), 1)
        gt_p = partner(gt_row // 16)
        gt_pick = ((gt_p // 4) * 16 + (gt_row % 4) * 4 + gt_p % 4) == gt_lane
        for v in range(Q):
            chosen = (g_pick & ((g_lane // 4) % 4 == v)).astype(F32).astype(BF16)
            top, low = split(toeplitz(row_of(v, 5), NZ, NZ, -HALF))
            nh[v] = dot(top, chosen).astype(BF16)
            nl[v] = dot(low, chosen).astype(BF16)
            chosen = (gt_pick & ((gt_row // 4) % 4 == v)).astype(F32).astype(BF16)
            top, low = split(toeplitz(row_of(v, 2), NZ, NZ, -HALF))
            nth[:, v * NZ : (v + 1) * NZ] = dot(chosen, top).astype(BF16)
            ntl[:, v * NZ : (v + 1) * NZ] = dot(chosen, low).astype(BF16)
            top, low = split(toeplitz(row_of(v, 1), Y, Y, -HALF))
            kyth[v] = top
            kytl[v] = low
            top, low = split(toeplitz(row_of(v, 4), Y, Y, -HALF))
            kyh[v] = top
            kyl[v] = low

    def halo(it, c):
        own = u.at[it, c, 1]
        remote(own, u.at[it, c, 2], halo_s.at[it, c, 0], halo_r.at[it, c, 0], dev(h, left, q)).start()
        remote(own, u.at[it, c, 0], halo_s.at[it, c, 1], halo_r.at[it, c, 1], dev(h, right, q)).start()
        drains.append(lambda: [wait_for(own, halo_s.at[it, c, k]) for k in range(2)])

    def halo_wait(it, c):
        wait_for(u.at[it, c, 2], halo_r.at[it, c, 0])
        wait_for(u.at[it, c, 0], halo_r.at[it, c, 1])

    def observed_second():
        a = zc // 8
        b = zc % 8

        def obs_second(d):
            hop = 8 + jnp.where((d + a + zc) % 2 == 0, d, -d - 1)
            t = (zc + hop) % RING
            hs = t // 2
            wait_for(o1.at[hs], o1_r.at[hs])

            @pl.when(t != zc)
            def _():
                remote(o1.at[hs], o2.at[b], o2_s, o2_r.at[b], dev(h, t, q)).start()

            @pl.when(t == zc)
            def _():
                pltpu.make_async_copy(o1.at[hs], o2.at[b], o2_r.at[b]).start()

        loop(0, GROUPS, obs_second)
        kept = (zc % 2 == zc // 8).astype(jnp.int32)
        drains.append(lambda: wait_bytes(GROUPS - kept, o1.at[0], o2_s))

    def forward_x(it, c):
        pair(xb, u[it, c].reshape(3 * NZ, LANES))

        def forward(k):
            at = pl.ds(pl.multiple_of(k * 128, 128), 128)
            s1[it, c, pl.ds(k * 8, 8)] = times_pair(mh[at], ml[at], xb).reshape(8, 16, LANES)
            send_plane(s1.at[it, c], r1.at[it, c], a1_s.at[it, c], a1_r.at[it, c], k * 8, 8)

        loop(0, 4, forward)
        drains.append(lambda: wait_for(s1.at[it, c, pl.ds(0, PLANE - 1)], a1_s.at[it, c]))

    def forward_wait(it, c):
        wait_for(r1.at[it, c], a1_r.at[it, c])

    def forward_z(it, c):
        pair(zb, r1[it, c].reshape(ROWS, LANES))

        def blur_view(v):
            top, low = split(times_pair(nh[v], nl[v], zb))
            ztop[v, :, c * LANES : (c + 1) * LANES] = top
            zlow[v, :, c * LANES : (c + 1) * LANES] = low

        loop(0, Q, blur_view)

    def observed_third():
        start = (zc + jnp.where(zc % 2 == 1 - zc // 8, 0, 4)) % 8
        def obs_third(i):
            b = (start + jnp.where(i % 2 == 0, i // 2, -(i // 2) - 1) + 8) % 8
            wait_for(o2.at[b], o2_r.at[b])

            def one(i):
                mine = (b == h) & (i == q)
                dst = ob.at[q, pl.ds(h * 16, 16)]

                @pl.when(jnp.logical_not(mine))
                def _():
                    remote(o2.at[b, i], dst, o3_s, o3_r, dev(b, zc, i)).start()

                @pl.when(mine)
                def _():
                    pltpu.make_async_copy(o2.at[b, i], dst, o3_r).start()

            loop(0, Q, one)

        loop(0, GROUPS, obs_third)
        drains.append(lambda: wait_bytes(PLANE - 1, o1.at[0, 0], o3_s))

    def observed_wait():
        wait_for(ob, o3_r)

    def quotient():
        def view(v):
            blur = dot3(ztop[v], zlow[v], kyth[v], kytl[v])
            top, low = split(ob[v] / blur)
            top, low = split(dot3(top, low, kyh[v], kyl[v]))
            at = pl.ds(pl.multiple_of(v * NZ, NZ), NZ)
            for c in range(CHUNKS):
                wb[c, at, 0:LANES] = top[:, c * LANES : (c + 1) * LANES]
                wb[c, at, LANES:] = low[:, c * LANES : (c + 1) * LANES]

        loop(0, Q, view)

    def backward_z(it, c):
        def backward(k):
            at = pl.ds(pl.multiple_of(k * 128, 128), 128)
            s2[it, c, pl.ds(k * 8, 8)] = times_pair(nth[at], ntl[at], wb.at[c]).reshape(8, 16, LANES)
            send_plane(s2.at[it, c], r2.at[it, c], a2_s.at[it, c], a2_r.at[it, c], k * 8, 8)

        loop(0, 4, backward)
        drains.append(lambda: wait_for(s2.at[it, c, pl.ds(0, PLANE - 1)], a2_s.at[it, c]))

    def backward_wait(it, c):
        wait_for(r2.at[it, c], a2_r.at[it, c])

    def backward_x(it, c):
        pair(zb, r2[it, c].reshape(ROWS, LANES))

        def piece(k):
            return times_pair(mth[k * NZ : (k + 1) * NZ], mtl[k * NZ : (k + 1) * NZ], zb)

        back[it, c, 0] = piece(0)
        remote(back.at[it, c, 0], back.at[it, c, 4], bk_s.at[it, c, 0], bk_r.at[it, c, 0], dev(h, left, q)).start()
        back[it, c, 2] = piece(2)
        remote(back.at[it, c, 2], back.at[it, c, 3], bk_s.at[it, c, 1], bk_r.at[it, c, 1], dev(h, right, q)).start()
        back[it, c, 1] = piece(1)
        drains.append(lambda: [wait_for(back.at[it, c, 0], bk_s.at[it, c, k]) for k in range(2)])

    def back_wait(it, c):
        wait_for(back.at[it, c, 4], bk_r.at[it, c, 0])
        wait_for(back.at[it, c, 3], bk_r.at[it, c, 1])

    def update(it, c):
        u[it + 1, c, 1] = u[it, c, 1] * (back[it, c, 1] + back[it, c, 3] + back[it, c, 4]) * (1.0 / Q)

    def send_out(c):
        def one(i):
            j = (zc // 4 + i + 1) % J
            t = 4 * j + q
            src = u.at[ITERS, c, 1, pl.ds(j * 32, 32)]
            dst = out.at[0, pl.ds(zc * 32, 32), lanes(c)]

            @pl.when(t != zc)
            def _():
                remote(src, dst, uo_s.at[c], uo_r.at[c], dev(h, t, q)).start()

            @pl.when(t == zc)
            def _():
                pltpu.make_async_copy(src, dst, uo_r.at[c]).start()

        loop(0, J, one)
        kept = (zc % Q == q).astype(jnp.int32)
        drains.append(lambda: wait_bytes(J - kept, u.at[ITERS, c, 1, pl.ds(0, 32)], uo_s.at[c]))

    home = zc % Q
    role = q ^ home

    def pass_out(c):
        part = out.at[0, :, lanes(c)]

        @pl.when(role == 0)
        def _():
            wait_for(part, uo_r.at[c])
            remote(part, part, fw_s.at[c, 0], fa_r.at[c], dev(h, zc, q ^ 2)).start()
            remote(part, part, fw_s.at[c, 1], fb_r.at[c], dev(h, zc, q ^ 1)).start()

        @pl.when(role == 2)
        def _():
            wait_for(part, fa_r.at[c])
            remote(part, part, fw_s.at[c, 1], fb_r.at[c], dev(h, zc, q ^ 1)).start()

        def drain():
            @pl.when(role == 0)
            def _():
                wait_for(part, fw_s.at[c, 0])
                wait_for(part, fw_s.at[c, 1])

            @pl.when(role == 2)
            def _():
                wait_for(part, fw_s.at[c, 1])

            @pl.when((role == 1) | (role == 3))
            def _():
                wait_for(part, fb_r.at[c])

        drains.append(drain)

    phases = [(estimate_in,), (observed_first,), (taps_out,), (matrices,), (observed_second,)]
    for c in range(CHUNKS):
        phases += [(estimate_wait, c), (halo, 0, c)]
    for c in range(CHUNKS):
        phases += [(halo_wait, 0, c), (forward_x, 0, c)]
    for c in range(CHUNKS):
        phases += [(forward_wait, 0, c), (forward_z, 0, c)]
    phases += [(observed_third,), (observed_wait,)]
    for it in range(ITERS):
        phases.append((quotient,))
        steps = [[(backward_z, it)], [(backward_wait, it), (backward_x, it)]]
        if it + 1 < ITERS:
            steps += [
                [(back_wait, it), (update, it), (halo, it + 1)],
                [(halo_wait, it + 1), (forward_x, it + 1)],
                [(forward_wait, it + 1), (forward_z, it + 1)],
            ]
        else:
            steps += [[(back_wait, it), (update, it), (send_out,)], [(pass_out,)]]
        order = sorted((n - 1 + c if n else -1, n, c) for n in range(len(steps)) for c in range(CHUNKS))
        for _, n, c in order:
            phases += [(*phase, c) for phase in steps[n]]
    for phase, *args in phases:
        phase(*args)
    for done in drains:
        done()


def per_device(estimate, observed, psf_x, psf_y, psf_z):
    rows = jnp.concatenate([psf_x, psf_y, psf_z], axis=0)
    rows = jnp.concatenate([rows, jnp.flip(rows, axis=1)], axis=0)
    psf = jnp.pad(rows, ((0, 2), (0, 128 - TAPS)))
    recorded = jnp.transpose(observed[0], (1, 0, 2))
    vmem = pl.BlockSpec(memory_space=pltpu.VMEM)
    sem = pltpu.SemaphoreType.DMA
    return pl.pallas_call(
        kernel,
        out_shape=jax.ShapeDtypeStruct((1, 512, Y), F32),
        in_specs=[vmem] * 3,
        out_specs=vmem,
        scratch_shapes=[
            pltpu.VMEM((Q, 8, 128), F32),
            pltpu.VMEM((ROWS, Y), BF16),
            pltpu.VMEM((ROWS, Y), BF16),
            pltpu.VMEM((Y, ROWS), BF16),
            pltpu.VMEM((Y, ROWS), BF16),
            pltpu.VMEM((Q, NZ, ROWS), BF16),
            pltpu.VMEM((Q, NZ, ROWS), BF16),
            pltpu.VMEM((ROWS, Q * NZ), BF16),
            pltpu.VMEM((ROWS, Q * NZ), BF16),
            pltpu.VMEM((Q, Y, Y), BF16),
            pltpu.VMEM((Q, Y, Y), BF16),
            pltpu.VMEM((Q, Y, Y), BF16),
            pltpu.VMEM((Q, Y, Y), BF16),
            pltpu.VMEM((ITERS + 1, CHUNKS, 3, NZ, LANES), F32),
            pltpu.VMEM((ITERS, CHUNKS, PLANE, 16, LANES), F32),
            pltpu.VMEM((ITERS, CHUNKS, PLANE, 16, LANES), F32),
            pltpu.VMEM((ITERS, CHUNKS, PLANE, 16, LANES), F32),
            pltpu.VMEM((ITERS, CHUNKS, PLANE, 16, LANES), F32),
            pltpu.VMEM((ITERS, CHUNKS, 5, NZ, LANES), F32),
            pltpu.VMEM((3 * NZ, 2 * LANES), BF16),
            pltpu.VMEM((ROWS, 2 * LANES), BF16),
            pltpu.VMEM((Q, NZ, Y), BF16),
            pltpu.VMEM((Q, NZ, Y), BF16),
            pltpu.VMEM((CHUNKS, ROWS, 2 * LANES), BF16),
            pltpu.VMEM((GROUPS, 4, 16, Y), F32),
            pltpu.VMEM((GROUPS, 4, 16, Y), F32),
            pltpu.VMEM((Q, NZ, Y), F32),
            sem, sem,
            sem, sem((CHUNKS,)),
            sem((ITERS, CHUNKS, 2)), sem((ITERS, CHUNKS, 2)),
            sem((ITERS, CHUNKS)), sem((ITERS, CHUNKS)),
            sem((ITERS, CHUNKS)), sem((ITERS, CHUNKS)),
            sem((ITERS, CHUNKS, 2)), sem((ITERS, CHUNKS, 2)),
            sem, sem((GROUPS,)),
            sem, sem((GROUPS,)),
            sem, sem,
            sem((CHUNKS,)), sem((CHUNKS,)),
            sem((CHUNKS, 2)), sem((CHUNKS,)), sem((CHUNKS,)),
        ],
        compiler_params=pltpu.CompilerParams(
            collective_id=0, has_side_effects=True, vmem_limit_bytes=48 * 1024 * 1024
        ),
    )(estimate[0], recorded, psf)


def solution(mesh):
    return jax.shard_map(
        per_device,
        mesh=mesh,
        in_specs=(
            P("wide", None, None),
            P("view", None, "wide", None),
            P("view", None),
            P("view", None),
            P("view", None),
        ),
        out_specs=P("wide", None, None),
        check_vma=False,
    )
```

```python
import functools

import jax
import jax.numpy as jnp
from jax import lax
from jax.experimental import pallas as pl
from jax.experimental.pallas import tpu as pltpu
from jax.sharding import PartitionSpec as P

TAPS = 63
HALF = (TAPS - 1) // 2
ITERS = 2
MESH = pl.DeviceIdType.MESH
F32 = jnp.float32
BF16 = jnp.bfloat16

RING = 16
GROUPS = 8
Q = 4
PLANE = GROUPS * Q
J = 4
Y = 384
NZ = 128
LANES = 128
CHUNKS = Y // LANES
FAR, NEAR = 0x2F5EB69A, 0x0C341D78
SELF = PLANE - 2
ROWS = PLANE * Q * J


def iota(shape, axis):
    return lax.broadcasted_iota(jnp.int32, shape, axis)


def split(value):
    top = value.astype(BF16)
    return top, (value - top.astype(F32)).astype(BF16)


def dot(a, b):
    return jnp.dot(a, b, preferred_element_type=F32)


def dot3(a_top, a_low, b_top, b_low):
    return dot(a_top, b_top) + (dot(a_top, b_low) + dot(a_low, b_top))


def toeplitz(row, rows, width, first):
    full = width + 128
    wide = jnp.concatenate([row, jnp.zeros((1, full - 128), F32)], axis=1)
    spread = jnp.broadcast_to(wide, (rows, full))
    return pltpu.roll(spread, first % full, axis=1, stride=1, stride_axis=0)[:, :width]


def kernel(
    est, obs, psf, out,
    taps, mh, ml, mth, mtl, nh, nl, nth, ntl, kyh, kyl, kyth, kytl,
    u, s1, r1, s2, r2, back, xb, zb, ztop, zlow, wb, o1, ob,
    psf_s, psf_r, uin_s, uin_r, halo_s, halo_r, a1_s, a1_r, a2_s, a2_r, bk_s, bk_r,
    o1_s, o1_r, o3_s, o3_r, uo_s, uo_r, fw_s, fa_r, fb_r,
):
    q = lax.axis_index("view")
    w = lax.axis_index("wide")
    h = w >> 4
    zc = w & 15
    p = h * Q + q
    x_at, y_at = h & 3, (h >> 2) * 2 + (q >> 1)

    def dev(hh, zz, qq):
        return {"view": qq, "wide": (hh << 4) | zz}

    def offset(k):
        step = k >> 1
        code = (jnp.where(step < 8, FAR, NEAR) >> ((step & 7) * 4)) & 15
        y = (y_at + (code >> 2)) & 3
        return (x_at + (code & 3)) & 3, y, ((y & 1) << 1) | ((q ^ k) & 1)

    def partner(k):
        x, y, view = offset(k)
        return ((y >> 1) << 4) | (x << 2) | view

    def partner_dev(k):
        x, y, view = offset(k)
        return {"view": view, "wide": ((y >> 1) << 6) | (x << 4) | zc}

    def remote(src, dst, send, recv, where):
        return pltpu.make_async_remote_copy(
            src_ref=src, dst_ref=dst, send_sem=send, recv_sem=recv, device_id=where, device_id_type=MESH
        )

    def wait_for(ref, sem):
        pltpu.make_async_copy(ref, ref, sem).wait()

    def loop(low, high, body):
        lax.fori_loop(low, high, lambda i, c: (body(i), c)[1], 0)

    barrier = pltpu.get_barrier_semaphore()

    def greet_ring(d):
        pl.semaphore_signal(barrier, inc=1, device_id=dev(h, (zc + d) & 15, q), device_id_type=MESH)

    def greet_plane(d):
        pl.semaphore_signal(barrier, inc=1, device_id=partner_dev(d), device_id_type=MESH)

    loop(1, RING, greet_ring)
    loop(0, SELF, greet_plane)
    greet_plane(SELF + 1)

    from_self = (h == (zc & 7)) & ((zc & 1) == (zc >> 3))

    def greet_source(i):
        c, v = (h + (i >> 2)) & 7, (q + i) & 3

        @pl.when(jnp.logical_not(from_self & (i == 0)))
        def _():
            pl.semaphore_signal(barrier, inc=1, device_id=dev(c, (zc & 1) * 8 + h, v), device_id_type=MESH)

    loop(0, PLANE, greet_source)
    pl.semaphore_wait(barrier, RING - 1 + PLANE - 1 + PLANE - from_self.astype(jnp.int32))

    def wait_bytes(count, ref, sem):
        loop(0, count, lambda i: wait_for(ref, sem))

    drains = []
    owner = (zc & 3) == q
    left = (zc + RING - 1) & 15
    right = (zc + 1) & 15

    def send_plane(send_buf, recv_buf, send, recv, first, count):
        def one(k):
            remote(send_buf.at[k], recv_buf.at[p], send, recv, partner_dev(k)).start()

        last = first + count == PLANE
        loop(first, first + count - jnp.where(last, 2, 0), one)

        @pl.when(last)
        def _():
            pltpu.make_async_copy(send_buf.at[SELF], recv_buf.at[p], recv).start()
            one(SELF + 1)

    def lanes(c):
        return pl.ds(c * LANES, LANES)

    def pair(ref, value):
        top, low = split(value)
        ref[:, 0:LANES] = top
        ref[:, LANES:] = low

    def times_pair(a_top, a_low, ref):
        got = dot(a_top, ref[...])
        return got[:, 0:LANES] + (got[:, LANES:] + dot(a_low, ref[:, 0:LANES]))

    def taps_out():
        def send_taps(d):
            remote(psf, taps.at[q], psf_s, psf_r, dev(h, zc, (q + d) & 3)).start()

        loop(1, Q, send_taps)
        pltpu.make_async_copy(psf, taps.at[q], psf_r).start()
        drains.append(lambda: wait_bytes(Q - 1, psf, psf_s))

    def estimate_in():
        @pl.when(owner)
        def _():
            for c in range(CHUNKS):
                mine = u.at[0, c, 1, pl.ds((zc >> 2) * 32, 32)]

                def send(i):
                    t = (zc + 8 + (1 - 2 * (i & 1)) * (i >> 1)) & 15
                    remote(est.at[pl.ds(t * 32, 32), lanes(c)], mine, uin_s, uin_r.at[c], dev(h, t, q)).start()

                loop(1, RING, send)
                pltpu.make_async_copy(est.at[pl.ds(zc * 32, 32), lanes(c)], mine, uin_r.at[c]).start()

        def drain():
            @pl.when(owner)
            def _():
                wait_for(est.at[pl.ds(0, 480)], uin_s)

        drains.append(drain)

    def estimate_wait(c):
        wait_for(u.at[0, c, 1], uin_r.at[c])

    def observed_first():
        def obs_first(d):
            c = (h + d) & 7
            remote(obs.at[:, pl.ds(c * 16, 16)], o1.at[h], o1_s, o1_r.at[h], dev(c, zc, q)).start()

        loop(1, GROUPS, obs_first)
        pltpu.make_async_copy(obs.at[:, pl.ds(h * 16, 16)], o1.at[h], o1_r.at[h]).start()
        drains.append(lambda: wait_for(o1.at[pl.ds(0, GROUPS - 1)], o1_s))

    def matrices():
        wait_for(taps, psf_r)

        norm = []
        for v in range(Q):
            raw = taps[v]
            norm.append(raw / jnp.sum(raw, axis=1, keepdims=True))

        def row_of(v, r):
            return norm[v][r : r + 1, :]

        low_ok = zc != 0
        high_ok = zc != RING - 1
        t_mat = jnp.concatenate([toeplitz(row_of(v, 3), 32, 128, 1) for v in range(Q)], axis=0)
        k_lane = iota((128, 128), 1)
        t_mat = jnp.where(((k_lane >= 32) | low_ok) & ((k_lane < 64) | high_ok), t_mat, 0.0)
        k_row = iota((128, 128), 0)
        tt_mat = jnp.zeros((128, 128), F32)
        for v in range(Q):
            block = toeplitz(row_of(v, 0), 128, 128, 32 * v - 63)
            tt_mat = jnp.where((k_lane >> 5) == v, block, tt_mat)
        tt_mat = jnp.where(((k_row >= 32) | low_ok) & ((k_row < 64) | high_ok), tt_mat, 0.0)
        t_top, t_low = split(t_mat)
        tt_top, tt_low = split(tt_mat)
        r_row, r_lane = iota((ROWS, 128), 0), iota((ROWS, 128), 1)
        pick_rows = ((partner(r_row >> 4) + 32 * ((r_row >> 2) & 3)) == r_lane).astype(F32).astype(BF16)
        c_row, c_lane = iota((128, Y), 0), iota((128, Y), 1)
        pick_cols = ((c_lane >> 7) * 32 + (c_lane & 31) == c_row).astype(F32).astype(BF16)
        same_j = (iota((ROWS, Y), 0) & 3) == ((iota((ROWS, Y), 1) >> 5) & 3)
        for part, ref in ((t_top, mh), (t_low, ml)):
            rows = dot(pick_rows, part).astype(BF16)
            ref[...] = jnp.where(same_j, dot(rows, pick_cols), 0.0).astype(BF16)
        rt_row, rt_lane = iota((128, ROWS), 0), iota((128, ROWS), 1)
        pick_rows_t = (((rt_lane >> 4) + 32 * ((rt_lane >> 2) & 3)) == rt_row).astype(F32).astype(BF16)
        ct_row, ct_lane = iota((Y, 128), 0), iota((Y, 128), 1)
        pick_cols_t = ((ct_row >> 7) * 32 + (ct_row & 31) == ct_lane).astype(F32).astype(BF16)
        same_j_t = (iota((Y, ROWS), 1) & 3) == ((iota((Y, ROWS), 0) >> 5) & 3)
        for part, ref in ((tt_top, mth), (tt_low, mtl)):
            rows = dot(pick_cols_t, part).astype(BF16)
            ref[...] = jnp.where(same_j_t, dot(rows, pick_rows_t), 0.0).astype(BF16)
        g_row, g_lane = iota((128, ROWS), 0), iota((128, ROWS), 1)
        g_pick = ((g_lane >> 6) * 16 + (g_lane & 3) * 4 + ((g_lane >> 4) & 3)) == g_row
        gt_row, gt_lane = iota((ROWS, 128), 0), iota((ROWS, 128), 1)
        gt_p = partner(gt_row >> 4)
        gt_pick = ((gt_p >> 2) * 16 + (gt_row & 3) * 4 + (gt_p & 3)) == gt_lane
        for v in range(Q):
            chosen = (g_pick & (((g_lane >> 2) & 3) == v)).astype(F32).astype(BF16)
            top, low = split(toeplitz(row_of(v, 5), NZ, NZ, -HALF))
            nh[v] = dot(top, chosen).astype(BF16)
            nl[v] = dot(low, chosen).astype(BF16)
            chosen = (gt_pick & (((gt_row >> 2) & 3) == v)).astype(F32).astype(BF16)
            top, low = split(toeplitz(row_of(v, 2), NZ, NZ, -HALF))
            nth[:, v * NZ : (v + 1) * NZ] = dot(chosen, top).astype(BF16)
            ntl[:, v * NZ : (v + 1) * NZ] = dot(chosen, low).astype(BF16)
            top, low = split(toeplitz(row_of(v, 1), Y, Y, -HALF))
            kyth[v] = top
            kytl[v] = low
            top, low = split(toeplitz(row_of(v, 4), Y, Y, -HALF))
            kyh[v] = top
            kyl[v] = low

    def halo(it, c):
        own = u.at[it, c, 1]
        remote(own, u.at[it, c, 2], halo_s.at[it, c, 0], halo_r.at[it, c, 0], dev(h, left, q)).start()
        remote(own, u.at[it, c, 0], halo_s.at[it, c, 1], halo_r.at[it, c, 1], dev(h, right, q)).start()
        drains.append(lambda: [wait_for(own, halo_s.at[it, c, k]) for k in range(2)])

    def halo_wait(it, c):
        wait_for(u.at[it, c, 2], halo_r.at[it, c, 0])
        wait_for(u.at[it, c, 0], halo_r.at[it, c, 1])

    def observed_second():
        a = zc >> 3
        b = zc & 7
        dst = ob.at[q, pl.ds(h * 16, 16)]

        def obs_second(d):
            hop = 8 + jnp.where(((d + a + zc) & 1) == 0, d, -d - 1)
            t = (zc + hop) & 15
            hs = t >> 1
            wait_for(o1.at[hs], o1_r.at[hs])

            def one(k):
                i = (q + k) & 3
                mine = (b == h) & (t == zc) & (k == 0)

                @pl.when(jnp.logical_not(mine))
                def _():
                    remote(o1.at[hs, i], dst, o3_s, o3_r, dev(b, t, i)).start()

                @pl.when(mine)
                def _():
                    pltpu.make_async_copy(o1.at[hs, i], dst, o3_r).start()

            loop(0, Q, one)

        loop(0, GROUPS, obs_second)
        drains.append(lambda: wait_bytes(PLANE - from_self.astype(jnp.int32), o1.at[0, 0], o3_s))

    def forward_x(it, c):
        pair(xb, u[it, c].reshape(3 * NZ, LANES))

        def forward(k):
            at = pl.ds(pl.multiple_of(k * 128, 128), 128)
            s1[it, c, pl.ds(k * 8, 8)] = times_pair(mh[at], ml[at], xb).reshape(8, 16, LANES)
            send_plane(s1.at[it, c], r1.at[it, c], a1_s.at[it, c], a1_r.at[it, c], k * 8, 8)

        loop(0, 4, forward)
        drains.append(lambda: wait_for(s1.at[it, c, pl.ds(0, PLANE - 1)], a1_s.at[it, c]))

    def forward_wait(it, c):
        wait_for(r1.at[it, c], a1_r.at[it, c])

    def forward_z(it, c):
        pair(zb, r1[it, c].reshape(ROWS, LANES))

        def blur_view(v):
            top, low = split(times_pair(nh[v], nl[v], zb))
            ztop[v, :, c * LANES : (c + 1) * LANES] = top
            zlow[v, :, c * LANES : (c + 1) * LANES] = low

        loop(0, Q, blur_view)

    def observed_wait():
        wait_for(ob, o3_r)

    def quotient():
        def view(v):
            blur = dot3(ztop[v], zlow[v], kyth[v], kytl[v])
            top, low = split(ob[v] / blur)
            top, low = split(dot3(top, low, kyh[v], kyl[v]))
            at = pl.ds(pl.multiple_of(v * NZ, NZ), NZ)
            for c in range(CHUNKS):
                wb[c, at, 0:LANES] = top[:, c * LANES : (c + 1) * LANES]
                wb[c, at, LANES:] = low[:, c * LANES : (c + 1) * LANES]

        loop(0, Q, view)

    def backward_z(it, c):
        def backward(k):
            at = pl.ds(pl.multiple_of(k * 128, 128), 128)
            s2[it, c, pl.ds(k * 8, 8)] = times_pair(nth[at], ntl[at], wb.at[c]).reshape(8, 16, LANES)
            send_plane(s2.at[it, c], r2.at[it, c], a2_s.at[it, c], a2_r.at[it, c], k * 8, 8)

        loop(0, 4, backward)
        drains.append(lambda: wait_for(s2.at[it, c, pl.ds(0, PLANE - 1)], a2_s.at[it, c]))

    def backward_wait(it, c):
        wait_for(r2.at[it, c], a2_r.at[it, c])

    def backward_x(it, c):
        pair(zb, r2[it, c].reshape(ROWS, LANES))

        def piece(k):
            return times_pair(mth[k * NZ : (k + 1) * NZ], mtl[k * NZ : (k + 1) * NZ], zb)

        back[it, c, 0] = piece(0)
        remote(back.at[it, c, 0], back.at[it, c, 4], bk_s.at[it, c, 0], bk_r.at[it, c, 0], dev(h, left, q)).start()
        back[it, c, 2] = piece(2)
        remote(back.at[it, c, 2], back.at[it, c, 3], bk_s.at[it, c, 1], bk_r.at[it, c, 1], dev(h, right, q)).start()
        back[it, c, 1] = piece(1)
        drains.append(lambda: [wait_for(back.at[it, c, 0], bk_s.at[it, c, k]) for k in range(2)])

    def back_wait(it, c):
        wait_for(back.at[it, c, 4], bk_r.at[it, c, 0])
        wait_for(back.at[it, c, 3], bk_r.at[it, c, 1])

    def update(it, c):
        u[it + 1, c, 1] = u[it, c, 1] * (back[it, c, 1] + back[it, c, 3] + back[it, c, 4]) * (1.0 / Q)

    def send_out(c):
        def one(i):
            j = ((zc >> 2) + i + 1) & 3
            t = 4 * j + q
            src = u.at[ITERS, c, 1, pl.ds(j * 32, 32)]
            dst = out.at[0, pl.ds(zc * 32, 32), lanes(c)]

            @pl.when(t != zc)
            def _():
                remote(src, dst, uo_s.at[c], uo_r.at[c], dev(h, t, q)).start()

            @pl.when(t == zc)
            def _():
                pltpu.make_async_copy(src, dst, uo_r.at[c]).start()

        loop(0, J, one)
        kept = ((zc & 3) == q).astype(jnp.int32)
        drains.append(lambda: wait_bytes(J - kept, u.at[ITERS, c, 1, pl.ds(0, 32)], uo_s.at[c]))

    home = zc & 3
    role = q ^ home

    def pass_out(c):
        part = out.at[0, :, lanes(c)]

        @pl.when(role == 0)
        def _():
            wait_for(part, uo_r.at[c])
            remote(part, part, fw_s.at[c, 0], fa_r.at[c], dev(h, zc, q ^ 2)).start()
            remote(part, part, fw_s.at[c, 1], fb_r.at[c], dev(h, zc, q ^ 1)).start()

        @pl.when(role == 2)
        def _():
            wait_for(part, fa_r.at[c])
            remote(part, part, fw_s.at[c, 1], fb_r.at[c], dev(h, zc, q ^ 1)).start()

        def drain():
            @pl.when(role == 0)
            def _():
                wait_for(part, fw_s.at[c, 0])
                wait_for(part, fw_s.at[c, 1])

            @pl.when(role == 2)
            def _():
                wait_for(part, fw_s.at[c, 1])

            @pl.when((role == 1) | (role == 3))
            def _():
                wait_for(part, fb_r.at[c])

        drains.append(drain)

    phases = [(estimate_in,), (observed_first,), (taps_out,), (matrices,)]
    for c in range(CHUNKS):
        phases += [(estimate_wait, c), (halo, 0, c)]
    phases.append((observed_second,))
    for c in range(CHUNKS):
        phases += [(halo_wait, 0, c), (forward_x, 0, c)]
    for c in range(CHUNKS):
        phases += [(forward_wait, 0, c), (forward_z, 0, c)]
    phases.append((observed_wait,))
    for it in range(ITERS):
        phases.append((quotient,))
        steps = [[(backward_z, it)], [(backward_wait, it), (backward_x, it)]]
        if it + 1 < ITERS:
            steps += [
                [(back_wait, it), (update, it), (halo, it + 1)],
                [(halo_wait, it + 1), (forward_x, it + 1)],
                [(forward_wait, it + 1), (forward_z, it + 1)],
            ]
        else:
            steps += [[(back_wait, it), (update, it), (send_out,)], [(pass_out,)]]
        order = sorted((n - 1 + c if n else -1, n, c) for n in range(len(steps)) for c in range(CHUNKS))
        for _, n, c in order:
            phases += [(*phase, c) for phase in steps[n]]
    for phase, *args in phases:
        phase(*args)
    for done in drains:
        done()


def per_device(estimate, observed, psf_x, psf_y, psf_z):
    rows = jnp.concatenate([psf_x, psf_y, psf_z], axis=0)
    rows = jnp.concatenate([rows, jnp.flip(rows, axis=1)], axis=0)
    psf = jnp.pad(rows, ((0, 2), (0, 128 - TAPS)))
    recorded = jnp.transpose(observed[0], (1, 0, 2))
    vmem = pl.BlockSpec(memory_space=pltpu.VMEM)
    sem = pltpu.SemaphoreType.DMA
    return pl.pallas_call(
        kernel,
        out_shape=jax.ShapeDtypeStruct((1, 512, Y), F32),
        in_specs=[vmem] * 3,
        out_specs=vmem,
        scratch_shapes=[
            pltpu.VMEM((Q, 8, 128), F32),
            pltpu.VMEM((ROWS, Y), BF16),
            pltpu.VMEM((ROWS, Y), BF16),
            pltpu.VMEM((Y, ROWS), BF16),
            pltpu.VMEM((Y, ROWS), BF16),
            pltpu.VMEM((Q, NZ, ROWS), BF16),
            pltpu.VMEM((Q, NZ, ROWS), BF16),
            pltpu.VMEM((ROWS, Q * NZ), BF16),
            pltpu.VMEM((ROWS, Q * NZ), BF16),
            pltpu.VMEM((Q, Y, Y), BF16),
            pltpu.VMEM((Q, Y, Y), BF16),
            pltpu.VMEM((Q, Y, Y), BF16),
            pltpu.VMEM((Q, Y, Y), BF16),
            pltpu.VMEM((ITERS + 1, CHUNKS, 3, NZ, LANES), F32),
            pltpu.VMEM((ITERS, CHUNKS, PLANE, 16, LANES), F32),
            pltpu.VMEM((ITERS, CHUNKS, PLANE, 16, LANES), F32),
            pltpu.VMEM((ITERS, CHUNKS, PLANE, 16, LANES), F32),
            pltpu.VMEM((ITERS, CHUNKS, PLANE, 16, LANES), F32),
            pltpu.VMEM((ITERS, CHUNKS, 5, NZ, LANES), F32),
            pltpu.VMEM((3 * NZ, 2 * LANES), BF16),
            pltpu.VMEM((ROWS, 2 * LANES), BF16),
            pltpu.VMEM((Q, NZ, Y), BF16),
            pltpu.VMEM((Q, NZ, Y), BF16),
            pltpu.VMEM((CHUNKS, ROWS, 2 * LANES), BF16),
            pltpu.VMEM((GROUPS, 4, 16, Y), F32),
            pltpu.VMEM((Q, NZ, Y), F32),
            sem, sem,
            sem, sem((CHUNKS,)),
            sem((ITERS, CHUNKS, 2)), sem((ITERS, CHUNKS, 2)),
            sem((ITERS, CHUNKS)), sem((ITERS, CHUNKS)),
            sem((ITERS, CHUNKS)), sem((ITERS, CHUNKS)),
            sem((ITERS, CHUNKS, 2)), sem((ITERS, CHUNKS, 2)),
            sem, sem((GROUPS,)),
            sem, sem,
            sem((CHUNKS,)), sem((CHUNKS,)),
            sem((CHUNKS, 2)), sem((CHUNKS,)), sem((CHUNKS,)),
        ],
        compiler_params=pltpu.CompilerParams(
            collective_id=0, has_side_effects=True, vmem_limit_bytes=48 * 1024 * 1024
        ),
    )(estimate[0], recorded, psf)


def solution(mesh):
    return jax.shard_map(
        per_device,
        mesh=mesh,
        in_specs=(
            P("wide", None, None),
            P("view", None, "wide", None),
            P("view", None),
            P("view", None),
            P("view", None),
        ),
        out_specs=P("wide", None, None),
        check_vma=False,
    )
```

```python
import functools

import jax
import jax.numpy as jnp
from jax import lax
from jax.experimental import pallas as pl
from jax.experimental.pallas import tpu as pltpu
from jax.sharding import PartitionSpec as P

TAPS = 63
HALF = (TAPS - 1) // 2
ITERS = 2
MESH = pl.DeviceIdType.MESH
F32 = jnp.float32
BF16 = jnp.bfloat16

RING = 16
GROUPS = 8
Q = 4
PLANE = GROUPS * Q
J = 4
Y = 384
NZ = 128
LANES = 128
CHUNKS = Y // LANES
FAR, NEAR = 0x2F5EB69A, 0x0C341D78
SELF = PLANE - 2
ROWS = PLANE * Q * J


def iota(shape, axis):
    return lax.broadcasted_iota(jnp.int32, shape, axis)


def split(value):
    top = value.astype(BF16)
    return top, (value - top.astype(F32)).astype(BF16)


def dot(a, b):
    return jnp.dot(a, b, preferred_element_type=F32)


def dot3(a_top, a_low, b_top, b_low):
    return dot(a_top, b_top) + (dot(a_top, b_low) + dot(a_low, b_top))


def toeplitz(row, rows, width, first):
    full = width + 128
    wide = jnp.concatenate([row, jnp.zeros((1, full - 128), F32)], axis=1)
    spread = jnp.broadcast_to(wide, (rows, full))
    return pltpu.roll(spread, first % full, axis=1, stride=1, stride_axis=0)[:, :width]


def kernel(
    est, obs, psf, out,
    taps, mh, ml, mth, mtl, nh, nl, nth, ntl, kyh, kyl, kyth, kytl,
    u, s1, r1, s2, r2, back, xb, zb, ztop, zlow, wb, blur, o1, ob,
    psf_s, psf_r, uin_s, uin_r, halo_s, halo_r, a1_s, a1_r, a2_s, a2_r, bk_s, bk_r,
    o1_s, o1_r, o3_s, o3_r, uo_s, uo_r, fw_s, fa_r, fb_r,
):
    q = lax.axis_index("view")
    w = lax.axis_index("wide")
    h = w >> 4
    zc = w & 15
    p = h * Q + q
    x_at, y_at = h & 3, (h >> 2) * 2 + (q >> 1)

    def dev(hh, zz, qq):
        return {"view": qq, "wide": (hh << 4) | zz}

    def offset(k):
        step = k >> 1
        code = (jnp.where(step < 8, FAR, NEAR) >> ((step & 7) * 4)) & 15
        y = (y_at + (code >> 2)) & 3
        return (x_at + (code & 3)) & 3, y, ((y & 1) << 1) | ((q ^ k) & 1)

    def partner(k):
        x, y, view = offset(k)
        return ((y >> 1) << 4) | (x << 2) | view

    def partner_dev(k):
        x, y, view = offset(k)
        return {"view": view, "wide": ((y >> 1) << 6) | (x << 4) | zc}

    def remote(src, dst, send, recv, where):
        return pltpu.make_async_remote_copy(
            src_ref=src, dst_ref=dst, send_sem=send, recv_sem=recv, device_id=where, device_id_type=MESH
        )

    def wait_for(ref, sem):
        pltpu.make_async_copy(ref, ref, sem).wait()

    def loop(low, high, body):
        lax.fori_loop(low, high, lambda i, c: (body(i), c)[1], 0)

    barrier = pltpu.get_barrier_semaphore()

    def greet_ring(d):
        pl.semaphore_signal(barrier, inc=1, device_id=dev(h, (zc + d) & 15, q), device_id_type=MESH)

    def greet_plane(d):
        pl.semaphore_signal(barrier, inc=1, device_id=partner_dev(d), device_id_type=MESH)

    loop(1, RING, greet_ring)
    loop(0, SELF, greet_plane)
    greet_plane(SELF + 1)

    from_self = (h == (zc & 7)) & ((zc & 1) == (zc >> 3))

    def greet_source(i):
        c, v = (h + (i >> 2)) & 7, (q + i) & 3

        @pl.when(jnp.logical_not(from_self & (i == 0)))
        def _():
            pl.semaphore_signal(barrier, inc=1, device_id=dev(c, (zc & 1) * 8 + h, v), device_id_type=MESH)

    loop(0, PLANE, greet_source)
    pl.semaphore_wait(barrier, RING - 1 + PLANE - 1 + PLANE - from_self.astype(jnp.int32))

    def wait_bytes(count, ref, sem):
        loop(0, count, lambda i: wait_for(ref, sem))

    drains = []
    owner = (zc & 3) == q
    left = (zc + RING - 1) & 15
    right = (zc + 1) & 15

    def send_plane(send_buf, recv_buf, send, recv):
        def one(k):
            remote(send_buf.at[k], recv_buf.at[p], send, recv, partner_dev(k)).start()

        loop(0, SELF, one)
        one(SELF + 1)
        pltpu.make_async_copy(send_buf.at[SELF], recv_buf.at[p], recv).start()

    def lanes(c):
        return pl.ds(c * LANES, LANES)

    def pair(ref, value):
        top, low = split(value)
        ref[:, 0:LANES] = top
        ref[:, LANES:] = low

    def times_pair(a_top, a_low, ref):
        got = dot(a_top, ref[...])
        return got[:, 0:LANES] + (got[:, LANES:] + dot(a_low, ref[:, 0:LANES]))

    def taps_out():
        def send_taps(d):
            remote(psf, taps.at[q], psf_s, psf_r, dev(h, zc, (q + d) & 3)).start()

        loop(1, Q, send_taps)
        pltpu.make_async_copy(psf, taps.at[q], psf_r).start()
        drains.append(lambda: wait_bytes(Q - 1, psf, psf_s))

    def estimate_in():
        @pl.when(owner)
        def _():
            for c in range(CHUNKS):
                mine = u.at[0, c, 1, pl.ds((zc >> 2) * 32, 32)]

                def send(i):
                    t = (zc + 8 + (1 - 2 * (i & 1)) * (i >> 1)) & 15
                    remote(est.at[pl.ds(t * 32, 32), lanes(c)], mine, uin_s, uin_r.at[c], dev(h, t, q)).start()

                loop(1, RING, send)
                pltpu.make_async_copy(est.at[pl.ds(zc * 32, 32), lanes(c)], mine, uin_r.at[c]).start()

        def drain():
            @pl.when(owner)
            def _():
                wait_for(est.at[pl.ds(0, 480)], uin_s)

        drains.append(drain)

    def estimate_wait(c):
        wait_for(u.at[0, c, 1], uin_r.at[c])

    def observed_first():
        def obs_first(d):
            c = (h + d) & 7
            remote(obs.at[:, pl.ds(c * 16, 16)], o1.at[h], o1_s, o1_r.at[h], dev(c, zc, q)).start()

        loop(1, GROUPS, obs_first)
        pltpu.make_async_copy(obs.at[:, pl.ds(h * 16, 16)], o1.at[h], o1_r.at[h]).start()
        drains.append(lambda: wait_for(o1.at[pl.ds(0, GROUPS - 1)], o1_s))

    def matrices():
        wait_for(taps, psf_r)

        norm = []
        for v in range(Q):
            raw = taps[v]
            norm.append(raw / jnp.sum(raw, axis=1, keepdims=True))

        def row_of(v, r):
            return norm[v][r : r + 1, :]

        low_ok = zc != 0
        high_ok = zc != RING - 1
        t_mat = jnp.concatenate([toeplitz(row_of(v, 3), 32, 128, 1) for v in range(Q)], axis=0)
        k_lane = iota((128, 128), 1)
        t_mat = jnp.where(((k_lane >= 32) | low_ok) & ((k_lane < 64) | high_ok), t_mat, 0.0)
        k_row = iota((128, 128), 0)
        tt_mat = jnp.zeros((128, 128), F32)
        for v in range(Q):
            block = toeplitz(row_of(v, 0), 128, 128, 32 * v - 63)
            tt_mat = jnp.where((k_lane >> 5) == v, block, tt_mat)
        tt_mat = jnp.where(((k_row >= 32) | low_ok) & ((k_row < 64) | high_ok), tt_mat, 0.0)
        t_top, t_low = split(t_mat)
        tt_top, tt_low = split(tt_mat)
        r_row, r_lane = iota((ROWS, 128), 0), iota((ROWS, 128), 1)
        pick_rows = ((partner(r_row >> 4) + 32 * ((r_row >> 2) & 3)) == r_lane).astype(F32).astype(BF16)
        c_row, c_lane = iota((128, Y), 0), iota((128, Y), 1)
        pick_cols = ((c_lane >> 7) * 32 + (c_lane & 31) == c_row).astype(F32).astype(BF16)
        same_j = (iota((ROWS, Y), 0) & 3) == ((iota((ROWS, Y), 1) >> 5) & 3)
        for part, ref in ((t_top, mh), (t_low, ml)):
            rows = dot(pick_rows, part).astype(BF16)
            ref[...] = jnp.where(same_j, dot(rows, pick_cols), 0.0).astype(BF16)
        rt_row, rt_lane = iota((128, ROWS), 0), iota((128, ROWS), 1)
        pick_rows_t = (((rt_lane >> 4) + 32 * ((rt_lane >> 2) & 3)) == rt_row).astype(F32).astype(BF16)
        ct_row, ct_lane = iota((Y, 128), 0), iota((Y, 128), 1)
        pick_cols_t = ((ct_row >> 7) * 32 + (ct_row & 31) == ct_lane).astype(F32).astype(BF16)
        same_j_t = (iota((Y, ROWS), 1) & 3) == ((iota((Y, ROWS), 0) >> 5) & 3)
        for part, ref in ((tt_top, mth), (tt_low, mtl)):
            rows = dot(pick_cols_t, part).astype(BF16)
            ref[...] = jnp.where(same_j_t, dot(rows, pick_rows_t), 0.0).astype(BF16)
        g_row, g_lane = iota((128, ROWS), 0), iota((128, ROWS), 1)
        g_pick = ((g_lane >> 6) * 16 + (g_lane & 3) * 4 + ((g_lane >> 4) & 3)) == g_row
        gt_row, gt_lane = iota((ROWS, 128), 0), iota((ROWS, 128), 1)
        gt_p = partner(gt_row >> 4)
        gt_pick = ((gt_p >> 2) * 16 + (gt_row & 3) * 4 + (gt_p & 3)) == gt_lane
        for v in range(Q):
            chosen = (g_pick & (((g_lane >> 2) & 3) == v)).astype(F32).astype(BF16)
            top, low = split(toeplitz(row_of(v, 5), NZ, NZ, -HALF))
            nh[v] = dot(top, chosen).astype(BF16)
            nl[v] = dot(low, chosen).astype(BF16)
            chosen = (gt_pick & (((gt_row >> 2) & 3) == v)).astype(F32).astype(BF16)
            top, low = split(toeplitz(row_of(v, 2), NZ, NZ, -HALF))
            nth[:, v * NZ : (v + 1) * NZ] = dot(chosen, top).astype(BF16)
            ntl[:, v * NZ : (v + 1) * NZ] = dot(chosen, low).astype(BF16)
            top, low = split(toeplitz(row_of(v, 1), Y, Y, -HALF))
            kyth[v] = top
            kytl[v] = low
            top, low = split(toeplitz(row_of(v, 4), Y, Y, -HALF))
            kyh[v] = top
            kyl[v] = low

    def halo(it, c):
        own = u.at[it, c, 1]
        remote(own, u.at[it, c, 2], halo_s.at[it, c, 0], halo_r.at[it, c, 0], dev(h, left, q)).start()
        remote(own, u.at[it, c, 0], halo_s.at[it, c, 1], halo_r.at[it, c, 1], dev(h, right, q)).start()
        drains.append(lambda: [wait_for(own, halo_s.at[it, c, k]) for k in range(2)])

    def halo_wait(it, c):
        wait_for(u.at[it, c, 2], halo_r.at[it, c, 0])
        wait_for(u.at[it, c, 0], halo_r.at[it, c, 1])

    def observed_second():
        a = zc >> 3
        b = zc & 7
        dst = ob.at[q, pl.ds(h * 16, 16)]

        def obs_second(d):
            hop = 8 + jnp.where(((d + a + zc) & 1) == 0, d, -d - 1)
            t = (zc + hop) & 15
            hs = t >> 1
            wait_for(o1.at[hs], o1_r.at[hs])

            def one(k):
                i = (q + k) & 3
                mine = (b == h) & (t == zc) & (k == 0)

                @pl.when(jnp.logical_not(mine))
                def _():
                    remote(o1.at[hs, i], dst, o3_s, o3_r, dev(b, t, i)).start()

                @pl.when(mine)
                def _():
                    pltpu.make_async_copy(o1.at[hs, i], dst, o3_r).start()

            loop(0, Q, one)

        loop(0, GROUPS, obs_second)
        drains.append(lambda: wait_bytes(PLANE - from_self.astype(jnp.int32), o1.at[0, 0], o3_s))

    def forward_x(it, c):
        pair(xb, u[it, c].reshape(3 * NZ, LANES))

        s1[it, c] = times_pair(mh[...], ml[...], xb).reshape(PLANE, 16, LANES)
        send_plane(s1.at[it, c], r1.at[it, c], a1_s.at[it, c], a1_r.at[it, c])
        drains.append(lambda: wait_for(s1.at[it, c, pl.ds(0, PLANE - 1)], a1_s.at[it, c]))

    def forward_wait(it, c):
        wait_for(r1.at[it, c], a1_r.at[it, c])

    def forward_z(it, c):
        pair(zb, r1[it, c].reshape(ROWS, LANES))

        rows = Q * NZ
        top, low = split(times_pair(nh[...].reshape(rows, ROWS), nl[...].reshape(rows, ROWS), zb))
        ztop[:, :, c * LANES : (c + 1) * LANES] = top.reshape(Q, NZ, LANES)
        zlow[:, :, c * LANES : (c + 1) * LANES] = low.reshape(Q, NZ, LANES)

    def observed_wait():
        wait_for(ob, o3_r)

    def forward_y():
        def view(v):
            blur[v] = dot3(ztop[v], zlow[v], kyth[v], kytl[v])

        loop(0, Q, view)

    def quotient():
        def view(v):
            top, low = split(ob[v] / blur[v])
            top, low = split(dot3(top, low, kyh[v], kyl[v]))
            at = pl.ds(pl.multiple_of(v * NZ, NZ), NZ)
            for c in range(CHUNKS):
                wb[c, at, 0:LANES] = top[:, c * LANES : (c + 1) * LANES]
                wb[c, at, LANES:] = low[:, c * LANES : (c + 1) * LANES]

        loop(0, Q, view)

    def backward_z(it, c):
        s2[it, c] = times_pair(nth[...], ntl[...], wb.at[c]).reshape(PLANE, 16, LANES)
        send_plane(s2.at[it, c], r2.at[it, c], a2_s.at[it, c], a2_r.at[it, c])
        drains.append(lambda: wait_for(s2.at[it, c, pl.ds(0, PLANE - 1)], a2_s.at[it, c]))

    def backward_wait(it, c):
        wait_for(r2.at[it, c], a2_r.at[it, c])

    def backward_x(it, c):
        pair(zb, r2[it, c].reshape(ROWS, LANES))

        def piece(k):
            return times_pair(mth[k * NZ : (k + 1) * NZ], mtl[k * NZ : (k + 1) * NZ], zb)

        back[it, c, 0] = piece(0)
        remote(back.at[it, c, 0], back.at[it, c, 4], bk_s.at[it, c, 0], bk_r.at[it, c, 0], dev(h, left, q)).start()
        back[it, c, 2] = piece(2)
        remote(back.at[it, c, 2], back.at[it, c, 3], bk_s.at[it, c, 1], bk_r.at[it, c, 1], dev(h, right, q)).start()
        back[it, c, 1] = piece(1)
        drains.append(lambda: [wait_for(back.at[it, c, 0], bk_s.at[it, c, k]) for k in range(2)])

    def back_wait(it, c):
        wait_for(back.at[it, c, 4], bk_r.at[it, c, 0])
        wait_for(back.at[it, c, 3], bk_r.at[it, c, 1])

    def update(it, c):
        u[it + 1, c, 1] = u[it, c, 1] * (back[it, c, 1] + back[it, c, 3] + back[it, c, 4]) * (1.0 / Q)

    def send_out(c):
        def one(i):
            j = ((zc >> 2) + i + 1) & 3
            t = 4 * j + q
            src = u.at[ITERS, c, 1, pl.ds(j * 32, 32)]
            dst = out.at[0, pl.ds(zc * 32, 32), lanes(c)]

            @pl.when(t != zc)
            def _():
                remote(src, dst, uo_s.at[c], uo_r.at[c], dev(h, t, q)).start()

            @pl.when(t == zc)
            def _():
                pltpu.make_async_copy(src, dst, uo_r.at[c]).start()

        loop(0, J, one)
        kept = ((zc & 3) == q).astype(jnp.int32)
        drains.append(lambda: wait_bytes(J - kept, u.at[ITERS, c, 1, pl.ds(0, 32)], uo_s.at[c]))

    home = zc & 3
    role = q ^ home

    def pass_out(c):
        part = out.at[0, :, lanes(c)]

        @pl.when(role == 0)
        def _():
            wait_for(part, uo_r.at[c])
            remote(part, part, fw_s.at[c, 0], fa_r.at[c], dev(h, zc, q ^ 2)).start()
            remote(part, part, fw_s.at[c, 1], fb_r.at[c], dev(h, zc, q ^ 1)).start()

        @pl.when(role == 2)
        def _():
            wait_for(part, fa_r.at[c])
            remote(part, part, fw_s.at[c, 1], fb_r.at[c], dev(h, zc, q ^ 1)).start()

        def drain():
            @pl.when(role == 0)
            def _():
                wait_for(part, fw_s.at[c, 0])
                wait_for(part, fw_s.at[c, 1])

            @pl.when(role == 2)
            def _():
                wait_for(part, fw_s.at[c, 1])

            @pl.when((role == 1) | (role == 3))
            def _():
                wait_for(part, fb_r.at[c])

        drains.append(drain)

    phases = [(taps_out,), (observed_first,), (estimate_in,), (matrices,)]
    for c in range(CHUNKS):
        phases += [(estimate_wait, c), (halo, 0, c)]
    phases.append((observed_second,))
    for c in range(CHUNKS):
        phases += [(halo_wait, 0, c), (forward_x, 0, c)]
    for c in range(CHUNKS):
        phases += [(forward_wait, 0, c), (forward_z, 0, c)]
    phases += [(forward_y,), (observed_wait,)]
    for it in range(ITERS):
        phases += [(quotient,)] if it == 0 else [(forward_y,), (quotient,)]
        steps = [[(backward_z, it)], [(backward_wait, it), (backward_x, it)]]
        if it + 1 < ITERS:
            steps += [
                [(back_wait, it), (update, it), (halo, it + 1)],
                [(halo_wait, it + 1), (forward_x, it + 1)],
                [(forward_wait, it + 1), (forward_z, it + 1)],
            ]
        else:
            steps += [[(back_wait, it), (update, it), (send_out,)], [(pass_out,)]]
        last = len(steps) - 1
        order = sorted((99 if n == last else n - 1 + c if n else -1, n, c) for n in range(last + 1) for c in range(CHUNKS))
        for _, n, c in order:
            phases += [(*phase, c) for phase in steps[n]]
    for phase, *args in phases:
        phase(*args)
    for done in drains:
        done()


def per_device(estimate, observed, psf_x, psf_y, psf_z):
    rows = jnp.concatenate([psf_x, psf_y, psf_z], axis=0)
    rows = jnp.concatenate([rows, jnp.flip(rows, axis=1)], axis=0)
    psf = jnp.pad(rows, ((0, 2), (0, 128 - TAPS)))
    recorded = jnp.transpose(observed[0], (1, 0, 2))
    vmem = pl.BlockSpec(memory_space=pltpu.VMEM)
    sem = pltpu.SemaphoreType.DMA
    return pl.pallas_call(
        kernel,
        out_shape=jax.ShapeDtypeStruct((1, 512, Y), F32),
        in_specs=[vmem] * 3,
        out_specs=vmem,
        scratch_shapes=[
            pltpu.VMEM((Q, 8, 128), F32),
            pltpu.VMEM((ROWS, Y), BF16),
            pltpu.VMEM((ROWS, Y), BF16),
            pltpu.VMEM((Y, ROWS), BF16),
            pltpu.VMEM((Y, ROWS), BF16),
            pltpu.VMEM((Q, NZ, ROWS), BF16),
            pltpu.VMEM((Q, NZ, ROWS), BF16),
            pltpu.VMEM((ROWS, Q * NZ), BF16),
            pltpu.VMEM((ROWS, Q * NZ), BF16),
            pltpu.VMEM((Q, Y, Y), BF16),
            pltpu.VMEM((Q, Y, Y), BF16),
            pltpu.VMEM((Q, Y, Y), BF16),
            pltpu.VMEM((Q, Y, Y), BF16),
            pltpu.VMEM((ITERS + 1, CHUNKS, 3, NZ, LANES), F32),
            pltpu.VMEM((ITERS, CHUNKS, PLANE, 16, LANES), F32),
            pltpu.VMEM((ITERS, CHUNKS, PLANE, 16, LANES), F32),
            pltpu.VMEM((ITERS, CHUNKS, PLANE, 16, LANES), F32),
            pltpu.VMEM((ITERS, CHUNKS, PLANE, 16, LANES), F32),
            pltpu.VMEM((ITERS, CHUNKS, 5, NZ, LANES), F32),
            pltpu.VMEM((3 * NZ, 2 * LANES), BF16),
            pltpu.VMEM((ROWS, 2 * LANES), BF16),
            pltpu.VMEM((Q, NZ, Y), BF16),
            pltpu.VMEM((Q, NZ, Y), BF16),
            pltpu.VMEM((CHUNKS, ROWS, 2 * LANES), BF16),
            pltpu.VMEM((Q, NZ, Y), F32),
            pltpu.VMEM((GROUPS, 4, 16, Y), F32),
            pltpu.VMEM((Q, NZ, Y), F32),
            sem, sem,
            sem, sem((CHUNKS,)),
            sem((ITERS, CHUNKS, 2)), sem((ITERS, CHUNKS, 2)),
            sem((ITERS, CHUNKS)), sem((ITERS, CHUNKS)),
            sem((ITERS, CHUNKS)), sem((ITERS, CHUNKS)),
            sem((ITERS, CHUNKS, 2)), sem((ITERS, CHUNKS, 2)),
            sem, sem((GROUPS,)),
            sem, sem,
            sem((CHUNKS,)), sem((CHUNKS,)),
            sem((CHUNKS, 2)), sem((CHUNKS,)), sem((CHUNKS,)),
        ],
        compiler_params=pltpu.CompilerParams(
            collective_id=0, has_side_effects=True, vmem_limit_bytes=48 * 1024 * 1024
        ),
    )(estimate[0], recorded, psf)


def solution(mesh):
    return jax.shard_map(
        per_device,
        mesh=mesh,
        in_specs=(
            P("wide", None, None),
            P("view", None, "wide", None),
            P("view", None),
            P("view", None),
            P("view", None),
        ),
        out_specs=P("wide", None, None),
        check_vma=False,
    )
```

```python
import functools

import jax
import jax.numpy as jnp
from jax import lax
from jax.experimental import pallas as pl
from jax.experimental.pallas import tpu as pltpu
from jax.sharding import PartitionSpec as P

TAPS = 63
HALF = (TAPS - 1) // 2
ITERS = 2
MESH = pl.DeviceIdType.MESH
F32 = jnp.float32
BF16 = jnp.bfloat16

RING = 16
GROUPS = 8
Q = 4
PLANE = GROUPS * Q
J = 4
Y = 384
NZ = 128
LANES = 128
CHUNKS = Y // LANES
FAR, NEAR = 0x2F5EB69A, 0x0C341D78
SELF = PLANE - 2
ROWS = PLANE * Q * J


def iota(shape, axis):
    return lax.broadcasted_iota(jnp.int32, shape, axis)


def split(value):
    top = value.astype(BF16)
    return top, (value - top.astype(F32)).astype(BF16)


def dot(a, b):
    return jnp.dot(a, b, preferred_element_type=F32)


def dot3(a_top, a_low, b_top, b_low):
    return dot(a_top, b_top) + (dot(a_top, b_low) + dot(a_low, b_top))


def toeplitz(row, rows, width, first):
    full = width + 128
    wide = jnp.concatenate([row, jnp.zeros((1, full - 128), F32)], axis=1)
    spread = jnp.broadcast_to(wide, (rows, full))
    return pltpu.roll(spread, first % full, axis=1, stride=1, stride_axis=0)[:, :width]


def kernel(
    est, obs, psf, out,
    taps, mh, ml, mth, mtl, nh, nl, nth, ntl, kyh, kyl, kyth, kytl,
    u, s1, r1, s2, r2, back, xb, zb, ztop, zlow, wb, blur, o1, ob,
    psf_s, psf_r, uin_s, uin_r, halo_s, halo_r, a1_s, a1_r, a2_s, a2_r, bk_s, bk_r,
    o1_s, o1_r, o3_s, o3_r, uo_s, uo_r, fw_s, fa_r, fb_r,
):
    q = lax.axis_index("view")
    w = lax.axis_index("wide")
    h = w >> 4
    zc = w & 15
    p = h * Q + q
    x_at, y_at = h & 3, (h >> 2) * 2 + (q >> 1)

    def dev(hh, zz, qq):
        return {"view": qq, "wide": (hh << 4) | zz}

    def offset(k):
        step = k >> 1
        code = (jnp.where(step < 8, FAR, NEAR) >> ((step & 7) * 4)) & 15
        y = (y_at + (code >> 2)) & 3
        return (x_at + (code & 3)) & 3, y, ((y & 1) << 1) | ((q ^ k) & 1)

    def partner(k):
        x, y, view = offset(k)
        return ((y >> 1) << 4) | (x << 2) | view

    def partner_dev(k):
        x, y, view = offset(k)
        return {"view": view, "wide": ((y >> 1) << 6) | (x << 4) | zc}

    def remote(src, dst, send, recv, where):
        return pltpu.make_async_remote_copy(
            src_ref=src, dst_ref=dst, send_sem=send, recv_sem=recv, device_id=where, device_id_type=MESH
        )

    def wait_for(ref, sem):
        pltpu.make_async_copy(ref, ref, sem).wait()

    def loop(low, high, body):
        lax.fori_loop(low, high, lambda i, c: (body(i), c)[1], 0)

    barrier = pltpu.get_barrier_semaphore()

    def greet_ring(d):
        pl.semaphore_signal(barrier, inc=1, device_id=dev(h, (zc + d) & 15, q), device_id_type=MESH)

    def greet_plane(d):
        pl.semaphore_signal(barrier, inc=1, device_id=partner_dev(d), device_id_type=MESH)

    loop(1, RING, greet_ring)
    loop(0, SELF, greet_plane)
    greet_plane(SELF + 1)

    from_self = (h == (zc & 7)) & ((zc & 1) == (zc >> 3))

    def greet_source(i):
        c, v = (h + (i >> 2)) & 7, (q + i) & 3

        @pl.when(jnp.logical_not(from_self & (i == 0)))
        def _():
            pl.semaphore_signal(barrier, inc=1, device_id=dev(c, (zc & 1) * 8 + h, v), device_id_type=MESH)

    loop(0, PLANE, greet_source)
    pl.semaphore_wait(barrier, RING - 1 + PLANE - 1 + PLANE - from_self.astype(jnp.int32))

    def wait_bytes(count, ref, sem):
        loop(0, count, lambda i: wait_for(ref, sem))

    drains = []
    owner = (zc & 3) == q
    left = (zc + RING - 1) & 15
    right = (zc + 1) & 15

    def send_plane(send_buf, recv_buf, send, recv):
        def one(k):
            remote(send_buf.at[k], recv_buf.at[p], send, recv, partner_dev(k)).start()

        loop(0, SELF, one)
        one(SELF + 1)
        pltpu.make_async_copy(send_buf.at[SELF], recv_buf.at[p], recv).start()

    def lanes(c):
        return pl.ds(c * LANES, LANES)

    def pair(ref, value):
        top, low = split(value)
        ref[:, 0:LANES] = top
        ref[:, LANES:] = low

    def times_pair(a_top, a_low, ref):
        got = dot(a_top, ref[...])
        return got[:, 0:LANES] + (got[:, LANES:] + dot(a_low, ref[:, 0:LANES]))

    def taps_out():
        def send_taps(d):
            remote(psf, taps.at[q], psf_s, psf_r, dev(h, zc, (q + d) & 3)).start()

        loop(1, Q, send_taps)
        pltpu.make_async_copy(psf, taps.at[q], psf_r).start()
        drains.append(lambda: wait_bytes(Q - 1, psf, psf_s))

    def estimate_in():
        @pl.when(owner)
        def _():
            for c in range(CHUNKS):
                mine = u.at[0, c, 1, pl.ds((zc >> 2) * 32, 32)]

                def send(i):
                    t = (zc + 8 + (1 - 2 * (i & 1)) * (i >> 1)) & 15
                    remote(est.at[pl.ds(t * 32, 32), lanes(c)], mine, uin_s, uin_r.at[c], dev(h, t, q)).start()

                loop(1, RING, send)
                pltpu.make_async_copy(est.at[pl.ds(zc * 32, 32), lanes(c)], mine, uin_r.at[c]).start()

        def drain():
            @pl.when(owner)
            def _():
                wait_for(est.at[pl.ds(0, 480)], uin_s)

        drains.append(drain)

    def estimate_wait(c):
        wait_for(u.at[0, c, 1], uin_r.at[c])

    def observed_first():
        def obs_first(d):
            c = (h + d) & 7
            remote(obs.at[:, pl.ds(c * 16, 16)], o1.at[h], o1_s, o1_r.at[h], dev(c, zc, q)).start()

        loop(1, GROUPS, obs_first)
        pltpu.make_async_copy(obs.at[:, pl.ds(h * 16, 16)], o1.at[h], o1_r.at[h]).start()
        drains.append(lambda: wait_for(o1.at[pl.ds(0, GROUPS - 1)], o1_s))

    def matrices():
        wait_for(taps, psf_r)

        norm = []
        for v in range(Q):
            raw = taps[v]
            norm.append(raw / jnp.sum(raw, axis=1, keepdims=True))

        def row_of(v, r):
            return norm[v][r : r + 1, :]

        low_ok = zc != 0
        high_ok = zc != RING - 1
        t_mat = jnp.concatenate([toeplitz(row_of(v, 3), 32, 128, 1) for v in range(Q)], axis=0)
        k_lane = iota((128, 128), 1)
        t_mat = jnp.where(((k_lane >= 32) | low_ok) & ((k_lane < 64) | high_ok), t_mat, 0.0)
        k_row = iota((128, 128), 0)
        tt_mat = jnp.zeros((128, 128), F32)
        for v in range(Q):
            block = toeplitz(row_of(v, 0), 128, 128, 32 * v - 63)
            tt_mat = jnp.where((k_lane >> 5) == v, block, tt_mat)
        tt_mat = jnp.where(((k_row >= 32) | low_ok) & ((k_row < 64) | high_ok), tt_mat, 0.0)
        t_top, t_low = split(t_mat)
        tt_top, tt_low = split(tt_mat)
        r_row, r_lane = iota((ROWS, 128), 0), iota((ROWS, 128), 1)
        pick_rows = ((partner(r_row >> 4) + 32 * ((r_row >> 2) & 3)) == r_lane).astype(F32).astype(BF16)
        c_row, c_lane = iota((128, Y), 0), iota((128, Y), 1)
        pick_cols = ((c_lane >> 7) * 32 + (c_lane & 31) == c_row).astype(F32).astype(BF16)
        same_j = (iota((ROWS, Y), 0) & 3) == ((iota((ROWS, Y), 1) >> 5) & 3)
        for part, ref in ((t_top, mh), (t_low, ml)):
            rows = dot(pick_rows, part).astype(BF16)
            ref[...] = jnp.where(same_j, dot(rows, pick_cols), 0.0).astype(BF16)
        rt_row, rt_lane = iota((128, ROWS), 0), iota((128, ROWS), 1)
        pick_rows_t = (((rt_lane >> 4) + 32 * ((rt_lane >> 2) & 3)) == rt_row).astype(F32).astype(BF16)
        ct_row, ct_lane = iota((Y, 128), 0), iota((Y, 128), 1)
        pick_cols_t = ((ct_row >> 7) * 32 + (ct_row & 31) == ct_lane).astype(F32).astype(BF16)
        same_j_t = (iota((Y, ROWS), 1) & 3) == ((iota((Y, ROWS), 0) >> 5) & 3)
        for part, ref in ((tt_top, mth), (tt_low, mtl)):
            rows = dot(pick_cols_t, part).astype(BF16)
            ref[...] = jnp.where(same_j_t, dot(rows, pick_rows_t), 0.0).astype(BF16)
        g_row, g_lane = iota((128, ROWS), 0), iota((128, ROWS), 1)
        g_pick = ((g_lane >> 6) * 16 + (g_lane & 3) * 4 + ((g_lane >> 4) & 3)) == g_row
        gt_row, gt_lane = iota((ROWS, 128), 0), iota((ROWS, 128), 1)
        gt_p = partner(gt_row >> 4)
        gt_pick = ((gt_p >> 2) * 16 + (gt_row & 3) * 4 + (gt_p & 3)) == gt_lane
        for v in range(Q):
            chosen = (g_pick & (((g_lane >> 2) & 3) == v)).astype(F32).astype(BF16)
            top, low = split(toeplitz(row_of(v, 5), NZ, NZ, -HALF))
            nh[v] = dot(top, chosen).astype(BF16)
            nl[v] = dot(low, chosen).astype(BF16)
            chosen = (gt_pick & (((gt_row >> 2) & 3) == v)).astype(F32).astype(BF16)
            top, low = split(toeplitz(row_of(v, 2), NZ, NZ, -HALF))
            nth[:, v * NZ : (v + 1) * NZ] = dot(chosen, top).astype(BF16)
            ntl[:, v * NZ : (v + 1) * NZ] = dot(chosen, low).astype(BF16)
            top, low = split(toeplitz(row_of(v, 1), Y, Y, -HALF))
            kyth[v] = top
            kytl[v] = low
            top, low = split(toeplitz(row_of(v, 4), Y, Y, -HALF))
            kyh[v] = top
            kyl[v] = low

    def halo(it, c):
        own = u.at[it, c, 1]
        remote(own, u.at[it, c, 2], halo_s.at[it, c, 0], halo_r.at[it, c, 0], dev(h, left, q)).start()
        remote(own, u.at[it, c, 0], halo_s.at[it, c, 1], halo_r.at[it, c, 1], dev(h, right, q)).start()
        drains.append(lambda: [wait_for(own, halo_s.at[it, c, k]) for k in range(2)])

    def halo_wait(it, c):
        wait_for(u.at[it, c, 2], halo_r.at[it, c, 0])
        wait_for(u.at[it, c, 0], halo_r.at[it, c, 1])

    def observed_second():
        a = zc >> 3
        b = zc & 7
        dst = ob.at[q, pl.ds(h * 16, 16)]

        def obs_second(d):
            hop = 8 + jnp.where(((d + a + zc) & 1) == 0, d, -d - 1)
            t = (zc + hop) & 15
            hs = t >> 1
            wait_for(o1.at[hs], o1_r.at[hs])

            def one(k):
                i = (q + k) & 3
                mine = (b == h) & (t == zc) & (k == 0)

                @pl.when(jnp.logical_not(mine))
                def _():
                    remote(o1.at[hs, i], dst, o3_s, o3_r, dev(b, t, i)).start()

                @pl.when(mine)
                def _():
                    pltpu.make_async_copy(o1.at[hs, i], dst, o3_r).start()

            loop(0, Q, one)

        loop(0, GROUPS, obs_second)
        drains.append(lambda: wait_bytes(PLANE - from_self.astype(jnp.int32), o1.at[0, 0], o3_s))

    def forward_x(it, c):
        pair(xb, u[it, c].reshape(3 * NZ, LANES))

        s1[it, c] = times_pair(mh[...], ml[...], xb).reshape(PLANE, 16, LANES)
        send_plane(s1.at[it, c], r1.at[it, c], a1_s.at[it, c], a1_r.at[it, c])
        drains.append(lambda: wait_for(s1.at[it, c, pl.ds(0, PLANE - 1)], a1_s.at[it, c]))

    def forward_wait(it, c):
        wait_for(r1.at[it, c], a1_r.at[it, c])

    def forward_z(it, c):
        pair(zb, r1[it, c].reshape(ROWS, LANES))

        rows = Q * NZ
        top, low = split(times_pair(nh[...].reshape(rows, ROWS), nl[...].reshape(rows, ROWS), zb))
        ztop[:, :, c * LANES : (c + 1) * LANES] = top.reshape(Q, NZ, LANES)
        zlow[:, :, c * LANES : (c + 1) * LANES] = low.reshape(Q, NZ, LANES)

    def observed_wait():
        wait_for(ob, o3_r)

    def forward_y():
        def view(v):
            blur[v] = dot3(ztop[v], zlow[v], kyth[v], kytl[v])

        loop(0, Q, view)

    def quotient():
        def view(v):
            top, low = split(ob[v] / blur[v])
            top, low = split(dot3(top, low, kyh[v], kyl[v]))
            at = pl.ds(pl.multiple_of(v * NZ, NZ), NZ)
            for c in range(CHUNKS):
                wb[c, at, 0:LANES] = top[:, c * LANES : (c + 1) * LANES]
                wb[c, at, LANES:] = low[:, c * LANES : (c + 1) * LANES]

        loop(0, Q, view)

    def backward_z(it, c):
        s2[it, c] = times_pair(nth[...], ntl[...], wb.at[c]).reshape(PLANE, 16, LANES)
        send_plane(s2.at[it, c], r2.at[it, c], a2_s.at[it, c], a2_r.at[it, c])
        drains.append(lambda: wait_for(s2.at[it, c, pl.ds(0, PLANE - 1)], a2_s.at[it, c]))

    def backward_wait(it, c):
        wait_for(r2.at[it, c], a2_r.at[it, c])

    def backward_x(it, c):
        pair(zb, r2[it, c].reshape(ROWS, LANES))

        def piece(k):
            return times_pair(mth[k * NZ : (k + 1) * NZ], mtl[k * NZ : (k + 1) * NZ], zb)

        back[it, c, 0] = piece(0)
        remote(back.at[it, c, 0], back.at[it, c, 4], bk_s.at[it, c, 0], bk_r.at[it, c, 0], dev(h, left, q)).start()
        back[it, c, 2] = piece(2)
        remote(back.at[it, c, 2], back.at[it, c, 3], bk_s.at[it, c, 1], bk_r.at[it, c, 1], dev(h, right, q)).start()
        back[it, c, 1] = piece(1)
        drains.append(lambda: [wait_for(back.at[it, c, 0], bk_s.at[it, c, k]) for k in range(2)])

    def back_wait(it, c):
        wait_for(back.at[it, c, 4], bk_r.at[it, c, 0])
        wait_for(back.at[it, c, 3], bk_r.at[it, c, 1])

    def update(it, c):
        u[it + 1, c, 1] = u[it, c, 1] * (back[it, c, 1] + back[it, c, 3] + back[it, c, 4]) * (1.0 / Q)

    def send_out(c):
        def one(i):
            j = ((zc >> 2) + i + 1) & 3
            t = 4 * j + q
            src = u.at[ITERS, c, 1, pl.ds(j * 32, 32)]
            dst = out.at[0, pl.ds(zc * 32, 32), lanes(c)]

            @pl.when(t != zc)
            def _():
                remote(src, dst, uo_s.at[c], uo_r.at[c, zc >> 3], dev(h, t, q)).start()

            @pl.when(t == zc)
            def _():
                pltpu.make_async_copy(src, dst, uo_r.at[c, zc >> 3]).start()

        loop(0, J, one)
        kept = ((zc & 3) == q).astype(jnp.int32)
        drains.append(lambda: wait_bytes(J - kept, u.at[ITERS, c, 1, pl.ds(0, 32)], uo_s.at[c]))

    home = zc & 3
    role = q ^ home

    def pass_out(c):
        part = out.at[0, :, lanes(c)]
        halves = [out.at[0, pl.ds(k * 256, 256), lanes(c)] for k in range(2)]

        @pl.when(role == 0)
        def _():
            for k, half in enumerate(halves):
                wait_for(half, uo_r.at[c, k])
                remote(half, half, fw_s.at[c, 0], fa_r.at[c, k], dev(h, zc, q ^ 2)).start()
                remote(half, half, fw_s.at[c, 1], fb_r.at[c, k], dev(h, zc, q ^ 1)).start()

        @pl.when(role == 2)
        def _():
            for k, half in enumerate(halves):
                wait_for(half, fa_r.at[c, k])
                remote(half, half, fw_s.at[c, 1], fb_r.at[c, k], dev(h, zc, q ^ 1)).start()

        def drain():
            @pl.when(role == 0)
            def _():
                wait_for(part, fw_s.at[c, 0])
                wait_for(part, fw_s.at[c, 1])

            @pl.when(role == 2)
            def _():
                wait_for(part, fw_s.at[c, 1])

            @pl.when((role == 1) | (role == 3))
            def _():
                for k, half in enumerate(halves):
                    wait_for(half, fb_r.at[c, k])

        drains.append(drain)

    phases = [(taps_out,), (observed_first,), (estimate_in,), (matrices,)]
    for c in range(CHUNKS):
        phases += [(estimate_wait, c), (halo, 0, c)]
    phases.append((observed_second,))
    for c in range(CHUNKS):
        phases += [(halo_wait, 0, c), (forward_x, 0, c)]
    for c in range(CHUNKS):
        phases += [(forward_wait, 0, c), (forward_z, 0, c)]
    phases += [(forward_y,), (observed_wait,)]
    for it in range(ITERS):
        phases += [(quotient,)] if it == 0 else [(forward_y,), (quotient,)]
        steps = [[(backward_z, it)], [(backward_wait, it), (backward_x, it)]]
        if it + 1 < ITERS:
            steps += [
                [(back_wait, it), (update, it), (halo, it + 1)],
                [(halo_wait, it + 1), (forward_x, it + 1)],
                [(forward_wait, it + 1), (forward_z, it + 1)],
            ]
        else:
            steps += [[(back_wait, it), (update, it), (send_out,)], [(pass_out,)]]
        last = len(steps) - 1
        order = sorted((99 if n == last else n - 1 + c if n else -1, n, c) for n in range(last + 1) for c in range(CHUNKS))
        for _, n, c in order:
            phases += [(*phase, c) for phase in steps[n]]
    for phase, *args in phases:
        phase(*args)
    for done in drains:
        done()


def per_device(estimate, observed, psf_x, psf_y, psf_z):
    rows = jnp.concatenate([psf_x, psf_y, psf_z], axis=0)
    rows = jnp.concatenate([rows, jnp.flip(rows, axis=1)], axis=0)
    psf = jnp.pad(rows, ((0, 2), (0, 128 - TAPS)))
    recorded = jnp.transpose(observed[0], (1, 0, 2))
    vmem = pl.BlockSpec(memory_space=pltpu.VMEM)
    sem = pltpu.SemaphoreType.DMA
    return pl.pallas_call(
        kernel,
        out_shape=jax.ShapeDtypeStruct((1, 512, Y), F32),
        in_specs=[vmem] * 3,
        out_specs=vmem,
        scratch_shapes=[
            pltpu.VMEM((Q, 8, 128), F32),
            pltpu.VMEM((ROWS, Y), BF16),
            pltpu.VMEM((ROWS, Y), BF16),
            pltpu.VMEM((Y, ROWS), BF16),
            pltpu.VMEM((Y, ROWS), BF16),
            pltpu.VMEM((Q, NZ, ROWS), BF16),
            pltpu.VMEM((Q, NZ, ROWS), BF16),
            pltpu.VMEM((ROWS, Q * NZ), BF16),
            pltpu.VMEM((ROWS, Q * NZ), BF16),
            pltpu.VMEM((Q, Y, Y), BF16),
            pltpu.VMEM((Q, Y, Y), BF16),
            pltpu.VMEM((Q, Y, Y), BF16),
            pltpu.VMEM((Q, Y, Y), BF16),
            pltpu.VMEM((ITERS + 1, CHUNKS, 3, NZ, LANES), F32),
            pltpu.VMEM((ITERS, CHUNKS, PLANE, 16, LANES), F32),
            pltpu.VMEM((ITERS, CHUNKS, PLANE, 16, LANES), F32),
            pltpu.VMEM((ITERS, CHUNKS, PLANE, 16, LANES), F32),
            pltpu.VMEM((ITERS, CHUNKS, PLANE, 16, LANES), F32),
            pltpu.VMEM((ITERS, CHUNKS, 5, NZ, LANES), F32),
            pltpu.VMEM((3 * NZ, 2 * LANES), BF16),
            pltpu.VMEM((ROWS, 2 * LANES), BF16),
            pltpu.VMEM((Q, NZ, Y), BF16),
            pltpu.VMEM((Q, NZ, Y), BF16),
            pltpu.VMEM((CHUNKS, ROWS, 2 * LANES), BF16),
            pltpu.VMEM((Q, NZ, Y), F32),
            pltpu.VMEM((GROUPS, 4, 16, Y), F32),
            pltpu.VMEM((Q, NZ, Y), F32),
            sem, sem,
            sem, sem((CHUNKS,)),
            sem((ITERS, CHUNKS, 2)), sem((ITERS, CHUNKS, 2)),
            sem((ITERS, CHUNKS)), sem((ITERS, CHUNKS)),
            sem((ITERS, CHUNKS)), sem((ITERS, CHUNKS)),
            sem((ITERS, CHUNKS, 2)), sem((ITERS, CHUNKS, 2)),
            sem, sem((GROUPS,)),
            sem, sem,
            sem((CHUNKS,)), sem((CHUNKS, 2)),
            sem((CHUNKS, 2)), sem((CHUNKS, 2)), sem((CHUNKS, 2)),
        ],
        compiler_params=pltpu.CompilerParams(
            collective_id=0, has_side_effects=True, vmem_limit_bytes=48 * 1024 * 1024
        ),
    )(estimate[0], recorded, psf)


def solution(mesh):
    return jax.shard_map(
        per_device,
        mesh=mesh,
        in_specs=(
            P("wide", None, None),
            P("view", None, "wide", None),
            P("view", None),
            P("view", None),
            P("view", None),
        ),
        out_specs=P("wide", None, None),
        check_vma=False,
    )
```
